512 devices in a mesh: section: 2 (over x_hi), row: 16 (over z, core), col: 16 (over y, x_lo).
Axes of the slice: x: 4 (x_hi: 2, x_lo: 2; x = x_hi * 2 + x_lo), y: 8, z: 8, core: 2. Of those that a mesh axis runs over, the one named last changes fastest.
Arguments:
- ends: bfloat16 [2, 512, 12288], P('section', 'col', 'row'), may hold values from -6 to 6
- weights: bfloat16 [2, 12288, 12288], P('section', 'row', 'col'), may hold values from -0.0546875 to 0.0546875
- routes: int32 [16, 16], P('row'), may hold values 0 or 1
Outputs:
- ends_out: bfloat16 [2, 512, 12288], P('section', 'col', 'row')
- weight_grads: bfloat16 [2, 12288, 12288], P('section', 'row', 'col')
The draws below stay inside these ranges and needn't reach their ends.
All inputs are finite; a program needn't handle non-finite values. No bound on the sum of `routes` on one device may be relied on, other than what follows from the above.
Results may differ from the reference program's by a relative error of at most 0.038.
Values may be sent and summed in bfloat16 or wider, within the bound.
A program may use at most 64 MiB of HBM per device.

```python
import jax
import jax.numpy as jnp
from jax import lax

D = 12288
TOKENS = 512
D_DEV = 768
N_ROW = 16
N_COL = 16


def place_ends(values, rng, low, largest):
    longest = values.shape.index(max(values.shape))
    spots = []
    for shift in (0, 1):
        where = [jax.random.randint(jax.random.fold_in(rng, axis), (), 0, length) for axis, length in enumerate(values.shape)]
        where[longest] = (where[longest] + shift) % values.shape[longest]
        spots.append(tuple(where))
    return values.at[spots[0]].set(low).at[spots[1]].set(largest)


def steps_of(stream_key, extent, cuts, smallest, largest):
    level = 1.0
    for position, parts in cuts:
        steps = jax.random.uniform(jax.random.fold_in(jax.random.fold_in(stream_key, 6), position), (parts,), jnp.float32, smallest / len(cuts), largest / len(cuts))
        level = level * jnp.repeat(jnp.exp(steps), extent[position] // parts).reshape((-1,) + (1,) * (len(extent) - 1 - position))
    return level


def bell_draw(rng, dims, scale, most, shards=(), kind=jnp.bfloat16):
    values = jax.random.normal(rng, dims, jnp.float32) * scale
    if len(shards) > 0:
        values = steps_of(rng, dims, shards, -0.22, 0.18) * values
    return jnp.clip(values, min=-most, max=most).astype(kind)


def setup_inputs(seed: int = 0) -> dict:
    key_list = jax.random.split(jax.random.key(seed), 4)
    ends = bell_draw(key_list[0], (2, TOKENS, D), 1.0, 6.0, ((0, 2), (1, 16), (2, 16)))
    weights = bell_draw(key_list[1], (2, D, D), D ** -0.5, 0.0546875, ((0, 2), (1, 16), (2, 16)))
    routes = place_ends((jax.random.randint(key_list[2], (N_ROW, N_COL), 0, 2) < 1).astype(jnp.int32), jax.random.fold_in(key_list[2], 1), 0, 1)
    return dict(ends=ends, weights=weights, routes=routes)


def gelu_pair(pre_act):
    values, backward = jax.vjp(jax.nn.gelu, pre_act)
    return (values, backward(jnp.ones_like(pre_act))[0])

def blockwise_first(inputs, w_first):
    tokens = inputs.shape[0]
    width = inputs.shape[1]

    def add_block(running, block_index):
        columns = lax.dynamic_slice_in_dim(inputs, block_index * D_DEV, D_DEV, 1)
        weight_rows = lax.dynamic_slice_in_dim(w_first, block_index * D_DEV, D_DEV, 0)
        block_part = jnp.dot(columns, weight_rows, preferred_element_type=jnp.float32).astype(jnp.bfloat16)
        block_part = lax.optimization_barrier(block_part)
        return (running + block_part.astype(jnp.float32), None)
    return lax.scan(add_block, jnp.zeros((tokens, width), jnp.float32), jnp.arange(width // D_DEV, dtype=jnp.int32))[0]

def blockwise_back(grad_pre, w_first):
    tokens = grad_pre.shape[0]
    width = grad_pre.shape[1]

    def add_block(running, block_index):
        columns = lax.dynamic_slice_in_dim(grad_pre, block_index * D_DEV, D_DEV, 1)
        weight_cols = lax.dynamic_slice_in_dim(w_first, block_index * D_DEV, D_DEV, 1)
        block_part = lax.dot_general(columns, weight_cols, (((1,), (1,)), ((), ())), preferred_element_type=jnp.float32).astype(jnp.bfloat16)
        block_part = lax.optimization_barrier(block_part)
        return (running + block_part.astype(jnp.float32), None)
    return lax.scan(add_block, jnp.zeros((tokens, width), jnp.float32), jnp.arange(width // D_DEV, dtype=jnp.int32))[0]

def reference(ends, weights, routes):
    inputs = ends[0]
    cotangent = ends[1]
    w_first = weights[0]
    w_second = weights[1]
    groups = routes.shape[1]
    tokens = inputs.shape[0]
    width = inputs.shape[1]
    block = tokens // groups
    group_width = width // groups
    pre_first = blockwise_first(inputs, w_first)
    hidden_full, slope_first = gelu_pair(pre_first)
    hidden = hidden_full.astype(jnp.bfloat16)
    route_rows = jnp.repeat(routes, block, axis=0)
    route_full = jnp.repeat(route_rows, group_width, axis=1).astype(jnp.float32)
    dense = lax.dot_general(hidden, w_second, (((1,), (1,)), ((), ())), preferred_element_type=jnp.float32)
    pre_second = dense * route_full
    out_second, slope_second = gelu_pair(pre_second)
    result_second = out_second.astype(jnp.bfloat16)
    grad_out = (cotangent.astype(jnp.float32) * slope_second).astype(jnp.bfloat16)
    masked_grad = (grad_out.astype(jnp.float32) * route_full).astype(jnp.bfloat16)
    grad_second = lax.dot_general(masked_grad, hidden, (((0,), (0,)), ((), ())), preferred_element_type=jnp.float32).astype(jnp.bfloat16)

    def add_group(running, group_index):
        columns = lax.dynamic_slice_in_dim(grad_out, group_index * group_width, group_width, 1)
        weight_rows = lax.dynamic_slice_in_dim(w_second, group_index * group_width, group_width, 0)
        group_part = jnp.dot(columns, weight_rows, preferred_element_type=jnp.float32).astype(jnp.bfloat16)
        group_part = lax.optimization_barrier(group_part)
        selector = lax.dynamic_slice_in_dim(route_rows, group_index, 1, 1).astype(jnp.float32)
        return (running + selector * group_part.astype(jnp.float32), None)
    grad_hidden = lax.scan(add_group, jnp.zeros((tokens, width), jnp.float32), jnp.arange(groups, dtype=jnp.int32))[0]
    grad_hidden = grad_hidden.astype(jnp.bfloat16)
    grad_pre = (grad_hidden.astype(jnp.float32) * slope_first).astype(jnp.bfloat16)
    grad_first = lax.dot_general(inputs, grad_pre, (((0,), (0,)), ((), ())), preferred_element_type=jnp.float32).astype(jnp.bfloat16)
    grad_inputs = blockwise_back(grad_pre, w_first).astype(jnp.bfloat16)
    return (jnp.stack([grad_inputs, result_second]), jnp.stack([grad_first, grad_second]))
```

```python
import functools
import math

import jax
import jax.numpy as jnp
from jax import lax
from jax.experimental import pallas as pl
from jax.experimental.pallas import tpu as pltpu
from jax.sharding import PartitionSpec as P

MESH = pl.DeviceIdType.MESH
HALVES = 2
ROWS = 16
TILE = 256
GELU_SCALE = math.sqrt(2.0 / math.pi)
GELU_CUBE = 0.044715


def gelu_pair(x):
    square = x * x
    t = jnp.tanh(GELU_SCALE * (x + GELU_CUBE * x * square))
    cdf = 0.5 * (1.0 + t)
    inner = GELU_SCALE * (1.0 + 3.0 * GELU_CUBE * square)
    return x * cdf, cdf + 0.5 * x * (1.0 - t * t) * inner


def rows_of(slot):
    return pl.ds(pl.multiple_of(slot * ROWS, ROWS), ROWS)


def offset_of(i, n):
    j = (i + 1) // 2
    return n // 2 + j * (1 - 2 * (i % 2))


class Line:
    def __init__(self, axis, n, place):
        self.n = n
        me = lax.axis_index(axis)
        self.pos = me // 2
        self.par = me % 2
        self.place = place

    def peer(self, pos):
        return self.place(pos * 2 + self.par)

    def sibling(self):
        return self.place(self.pos * 2 + 1 - self.par)

    def over_peers(self, body, near_first=False):
        def step(i, carry):
            k = self.n - 2 - i if near_first else i
            body(lax.rem(self.pos + offset_of(k, self.n), self.n))
            return carry

        lax.fori_loop(0, self.n - 1, step, 0)


def over(n, body):
    def step(i, carry):
        body(i)
        return carry

    lax.fori_loop(0, n, step, 0)


class Gather:
    def __init__(self, line, buf, ring_send, ring_recv, pair_send, pair_recv):
        self.line, self.buf = line, buf
        self.ring_send, self.ring_recv = ring_send, ring_recv
        self.pair_send, self.pair_recv = pair_send, pair_recv

    def own(self, h):
        line = self.line
        return self.buf.at[h, rows_of(line.par * line.n + line.pos)]

    def to_ring(self, h, pos):
        line = self.line
        return pltpu.make_async_remote_copy(
            src_ref=self.own(h), dst_ref=self.own(h),
            send_sem=self.ring_send.at[h, pos], recv_sem=self.ring_recv.at[h, line.pos],
            device_id=line.peer(pos), device_id_type=MESH)

    def from_ring(self, h, pos):
        line = self.line
        block = self.buf.at[h, rows_of(line.par * line.n + pos)]
        return pltpu.make_async_remote_copy(
            src_ref=block, dst_ref=block,
            send_sem=self.ring_send.at[h, pos], recv_sem=self.ring_recv.at[h, pos],
            device_id=line.peer(pos), device_id_type=MESH)

    def pair(self, h, par, pos):
        line = self.line
        block = self.buf.at[h, rows_of(par * line.n + pos)]
        return pltpu.make_async_remote_copy(
            src_ref=block, dst_ref=block,
            send_sem=self.pair_send.at[h, pos], recv_sem=self.pair_recv.at[h, pos],
            device_id=line.sibling(), device_id_type=MESH)

    def start(self, h):
        line = self.line
        line.over_peers(lambda pos: self.to_ring(h, pos).start())
        self.pair(h, line.par, line.pos).start()

    def finish(self, h):
        line = self.line

        def forward(pos):
            self.from_ring(h, pos).wait_recv()
            self.pair(h, line.par, pos).start()

        line.over_peers(forward, near_first=True)
        over(line.n, lambda pos: self.pair(h, 1 - line.par, pos).wait_recv())

    def drain(self, h):
        line = self.line
        line.over_peers(lambda pos: self.to_ring(h, pos).wait_send())
        over(line.n, lambda pos: self.pair(h, line.par, pos).wait_send())


class Scatter:
    def __init__(self, line, out, kept, got, both, land, pair_send, pair_recv, ring_send, ring_recv):
        self.line = line
        self.out, self.kept, self.got, self.both, self.land = out, kept, got, both, land
        self.pair_send, self.pair_recv = pair_send, pair_recv
        self.ring_send, self.ring_recv = ring_send, ring_recv

    def pair(self, h):
        return pltpu.make_async_remote_copy(
            src_ref=self.out.at[h], dst_ref=self.got.at[h],
            send_sem=self.pair_send.at[h], recv_sem=self.pair_recv.at[h],
            device_id=self.line.sibling(), device_id_type=MESH)

    def to_ring(self, h, pos):
        line = self.line
        return pltpu.make_async_remote_copy(
            src_ref=self.both.at[h, rows_of(pos)], dst_ref=self.land.at[h, rows_of(line.pos)],
            send_sem=self.ring_send.at[h, pos], recv_sem=self.ring_recv.at[h, line.pos],
            device_id=line.peer(pos), device_id_type=MESH)

    def from_ring(self, h, pos):
        line = self.line
        return pltpu.make_async_remote_copy(
            src_ref=self.both.at[h, rows_of(pos)], dst_ref=self.land.at[h, rows_of(pos)],
            send_sem=self.ring_send.at[h, pos], recv_sem=self.ring_recv.at[h, pos],
            device_id=line.peer(pos), device_id_type=MESH)

    def multiply(self, h, buf, w, transposed):
        line = self.line
        size = line.n * ROWS
        width = w.shape[0]
        tile = min(TILE, width)

        def product(par, store):
            left = buf[h, pl.ds(pl.multiple_of(par * size, size), size), :]

            def column(j):
                cut = pl.ds(pl.multiple_of(j * tile, tile), tile)
                if transposed:
                    store(cut, lax.dot_general(
                        left, w[cut, :], (((1,), (1,)), ((), ())), preferred_element_type=jnp.float32))
                else:
                    store(cut, jnp.dot(left, w[:, cut], preferred_element_type=jnp.float32))

            over(width // tile, column)

        def to_out(cut, value):
            self.out[h, :, cut] = value.astype(jnp.bfloat16)

        def to_kept(cut, value):
            self.kept[h, :, cut] = value

        product(1 - line.par, to_out)
        self.pair(h).start()
        product(line.par, to_kept)

    def combine(self, h):
        line = self.line
        self.pair(h).wait_recv()
        self.both[h] = (self.kept[h] + self.got[h].astype(jnp.float32)).astype(jnp.bfloat16)
        line.over_peers(lambda pos: self.to_ring(h, pos).start())

    def finish(self, h):
        line = self.line
        line.over_peers(lambda pos: self.from_ring(h, pos).wait_recv(), near_first=True)
        own = self.both[h, rows_of(line.pos), :]
        self.land[h, rows_of(line.pos), :] = own
        total = self.land[h, pl.ds(0, ROWS), :].astype(jnp.float32)
        for pos in range(1, line.n):
            total = total + self.land[h, pl.ds(pos * ROWS, ROWS), :].astype(jnp.float32)
        return total

    def drain(self, h):
        line = self.line
        self.pair(h).wait_send()
        line.over_peers(lambda pos: self.to_ring(h, pos).wait_send())


def kernel(n, ends_ref, w_hbm, routes_ref, ends_out, dw_hbm,
           w, col_buf, row_buf, dy, outgoing, incoming, slope, route_tiles, dw,
           rs_out, rs_kept, rs_got, rs_both, rs_land,
           ag_ring_send, ag_ring_recv, ag_pair_send, ag_pair_recv,
           rs_ring_send, rs_ring_recv, rs_pair_send, rs_pair_recv,
           cross_send, cross_recv, rt_send, rt_recv, rt_pair_send, rt_pair_recv, local_sem):
    s, r, c = lax.axis_index("section"), lax.axis_index("row"), lax.axis_index("col")
    row = Line("row", n, lambda i: (s, i, c))
    col = Line("col", n, lambda i: (s, r, i))
    over_there = (1 - s, r, c)

    ag_col = Gather(col, col_buf, ag_ring_send.at[0], ag_ring_recv.at[0], ag_pair_send.at[0], ag_pair_recv.at[0])
    ag_row = Gather(row, row_buf, ag_ring_send.at[1], ag_ring_recv.at[1], ag_pair_send.at[1], ag_pair_recv.at[1])

    def scatter(line, k):
        return Scatter(line, rs_out.at[k], rs_kept.at[k], rs_got.at[k], rs_both.at[k], rs_land.at[k],
                       rs_pair_send.at[k], rs_pair_recv.at[k], rs_ring_send.at[k], rs_ring_recv.at[k])

    rs_row, rs_col = scatter(row, 0), scatter(col, 1)

    def cross(h, dst):
        return pltpu.make_async_remote_copy(
            src_ref=outgoing.at[h], dst_ref=dst,
            send_sem=cross_send.at[h], recv_sem=cross_recv.at[h],
            device_id=over_there, device_id_type=MESH)

    load_w = pltpu.make_async_copy(w_hbm.at[0], w, local_sem.at[0])
    store_dw = pltpu.make_async_copy(dw, dw_hbm.at[0], local_sem.at[1])
    load_w.start()

    barrier = pltpu.get_barrier_semaphore()

    def greet(device):
        pl.semaphore_signal(barrier, inc=1, device_id=device, device_id_type=MESH)

    col.over_peers(lambda pos: greet(col.peer(pos)))
    greet(col.sibling())
    row.over_peers(lambda pos: greet(row.peer(pos)))
    greet(row.sibling())
    greet(over_there)

    def load_ends(h, dst):
        return pltpu.make_async_copy(ends_ref.at[0, pl.ds(h * ROWS, ROWS)], dst, local_sem.at[2 + h])

    def weight_grad():
        width = w.shape[0]
        tile = min(TILE, width)

        def block(k):
            at_row = pl.ds(pl.multiple_of((k // (width // tile)) * tile, tile), tile)
            at_col = pl.ds(pl.multiple_of((k % (width // tile)) * tile, tile), tile)
            total = jnp.zeros((tile, tile), jnp.float32)
            for h in range(HALVES):
                total = total + lax.dot_general(
                    col_buf[h, :, at_row], row_buf[h, :, at_col], (((0,), (0,)), ((), ())),
                    preferred_element_type=jnp.float32)
            dw[at_row, at_col] = total.astype(jnp.bfloat16)

        over((width // tile) ** 2, block)
        store_dw.start()

    def col_to_row():
        for h in range(HALVES):
            ag_col.finish(h)
            if h == 0:
                pl.when(s == 0)(load_w.wait)
            rs_row.multiply(h, col_buf, w, False)
            rs_row.combine(h)

    def row_to_col():
        for h in range(HALVES):
            ag_row.finish(h)
            if h == 0:
                pl.when(s == 1)(load_w.wait)
            rs_col.multiply(h, row_buf, w, True)
        for h in range(HALVES):
            rs_col.combine(h)

    halves = range(HALVES)

    @pl.when(s == 0)
    def _():
        for h in halves:
            load_ends(h, ag_col.own(h)).start()
        for h in halves:
            load_ends(h, ag_col.own(h)).wait()
        pl.semaphore_wait(barrier, 2 * (n - 1) + 3)
        for h in halves:
            ag_col.start(h)
        col_to_row()
        for h in halves:
            value, grad = gelu_pair(rs_row.finish(h))
            outgoing[h] = value.astype(jnp.bfloat16)
            cross(h, ag_row.own(h)).start()
            slope[h] = grad
        for h in halves:
            ag_col.drain(h)
            rs_row.drain(h)
        for h in halves:
            cross(h, incoming.at[h]).wait_recv()
            grad = incoming[h].astype(jnp.float32) * slope[h]
            ag_row.own(h)[...] = grad.astype(jnp.bfloat16)
            ag_row.start(h)
        row_to_col()
        weight_grad()
        for h in halves:
            ends_out[0, pl.ds(h * ROWS, ROWS), :] = rs_col.finish(h).astype(jnp.bfloat16)
        for h in halves:
            cross(h, ag_row.own(h)).wait_send()
            ag_row.drain(h)
            rs_col.drain(h)
        store_dw.wait()

    @pl.when(s == 1)
    def _():
        for h in halves:
            load_ends(h, dy.at[h]).start()
        route_tiles[row.par, row.pos] = jnp.zeros((8, 128), jnp.float32)
        route_tiles[row.par, row.pos, 0:1, 0:2 * n] = routes_ref[...].astype(jnp.float32)
        for h in halves:
            load_ends(h, dy.at[h]).wait()
        pl.semaphore_wait(barrier, 2 * (n - 1) + 3)

        def tile_to(pos):
            mine = route_tiles.at[row.par, row.pos]
            return pltpu.make_async_remote_copy(
                src_ref=mine, dst_ref=mine, send_sem=rt_send.at[pos], recv_sem=rt_recv.at[row.pos],
                device_id=row.peer(pos), device_id_type=MESH)

        def tile_from(pos):
            tile = route_tiles.at[row.par, pos]
            return pltpu.make_async_remote_copy(
                src_ref=tile, dst_ref=tile, send_sem=rt_send.at[pos], recv_sem=rt_recv.at[pos],
                device_id=row.peer(pos), device_id_type=MESH)

        def tiles(par):
            return pltpu.make_async_remote_copy(
                src_ref=route_tiles.at[par], dst_ref=route_tiles.at[par],
                send_sem=rt_pair_send.at[0], recv_sem=rt_pair_recv.at[0],
                device_id=row.sibling(), device_id_type=MESH)

        row.over_peers(lambda pos: tile_to(pos).start())
        row.over_peers(lambda pos: tile_from(pos).wait_recv())
        tiles(row.par).start()
        tiles(1 - row.par).wait_recv()
        row.over_peers(lambda pos: tile_to(pos).wait_send())
        tiles(row.par).wait_send()
        picked = route_tiles[col.par, col.pos, 0:1, :]
        lanes = lax.broadcasted_iota(jnp.int32, (1, 128), 1)
        routed = jnp.sum(jnp.where(lanes == r, picked, 0.0), axis=1, keepdims=True)

        for h in halves:
            cross(h, ag_row.own(h)).wait_recv()
            ag_row.start(h)
        row_to_col()
        for h in halves:
            value, grad = gelu_pair(rs_col.finish(h) * routed)
            masked = (dy[h].astype(jnp.float32) * grad).astype(jnp.bfloat16).astype(jnp.float32) * routed
            ag_col.own(h)[...] = masked.astype(jnp.bfloat16)
            ag_col.start(h)
            ends_out[0, pl.ds(h * ROWS, ROWS), :] = value.astype(jnp.bfloat16)
        col_to_row()
        for h in halves:
            outgoing[h] = rs_row.finish(h).astype(jnp.bfloat16)
            cross(h, incoming.at[h]).start()
        weight_grad()
        for h in halves:
            ag_col.drain(h)
            rs_row.drain(h)
            ag_row.drain(h)
            rs_col.drain(h)
            cross(h, incoming.at[h]).wait_send()
        store_dw.wait()


def shards(ends, weights, routes):
    width = weights.shape[1]
    n = lax.axis_size("row") // 2
    half = n * ROWS
    bf16, f32 = jnp.bfloat16, jnp.float32
    dma = pltpu.SemaphoreType.DMA
    anywhere = pl.BlockSpec(memory_space=pl.ANY)
    in_vmem = pl.BlockSpec(memory_space=pltpu.VMEM)
    return pl.pallas_call(
        functools.partial(kernel, n),
        out_shape=(jax.ShapeDtypeStruct(ends.shape, bf16), jax.ShapeDtypeStruct(weights.shape, bf16)),
        in_specs=[anywhere, anywhere, in_vmem],
        out_specs=(in_vmem, anywhere),
        scratch_shapes=[
            pltpu.VMEM((width, width), bf16),
            pltpu.VMEM((HALVES, 2 * half, width), bf16),
            pltpu.VMEM((HALVES, 2 * half, width), bf16),
            pltpu.VMEM((HALVES, ROWS, width), bf16),
            pltpu.VMEM((HALVES, ROWS, width), bf16),
            pltpu.VMEM((HALVES, ROWS, width), bf16),
            pltpu.VMEM((HALVES, ROWS, width), f32),
            pltpu.VMEM((2, n, 8, 128), f32),
            pltpu.VMEM((width, width), bf16),
            pltpu.VMEM((2, HALVES, half, width), bf16),
            pltpu.VMEM((2, HALVES, half, width), f32),
            pltpu.VMEM((2, HALVES, half, width), bf16),
            pltpu.VMEM((2, HALVES, half, width), bf16),
            pltpu.VMEM((2, HALVES, half, width), bf16),
            dma((2, HALVES, n)), dma((2, HALVES, n)), dma((2, HALVES, n)), dma((2, HALVES, n)),
            dma((2, HALVES, n)), dma((2, HALVES, n)), dma((2, HALVES)), dma((2, HALVES)),
            dma((HALVES,)), dma((HALVES,)), dma((n,)), dma((n,)), dma((1,)), dma((1,)), dma((4,)),
        ],
        compiler_params=pltpu.CompilerParams(
            collective_id=0, has_side_effects=True, vmem_limit_bytes=40 * 2**20),
        cost_estimate=pl.CostEstimate(
            flops=6 * half * 4 * width * width, bytes_accessed=4 * width * width, transcendentals=0),
    )(ends, weights, routes)


def solution(mesh):
    placed = (P("section", "col", "row"), P("section", "row", "col"), P("row", None))
    return jax.shard_map(
        shards,
        mesh=mesh,
        in_specs=placed,
        out_specs=(P("section", "col", "row"), P("section", "row", "col")),
        check_vma=False,
    )
```

```python
import functools
import math

import jax
import jax.numpy as jnp
from jax import lax
from jax.experimental import pallas as pl
from jax.experimental.pallas import tpu as pltpu
from jax.sharding import PartitionSpec as P

MESH = pl.DeviceIdType.MESH
HALVES = 2
ROWS = 16
TILE = 256
FAR_GATHER = 0
FAR_SUM = 0
FAR_CROSS = 0
WHOLE_ROW_PAIR = True
VMEM_LIMIT = 62 * 2**20
GELU_SCALE = math.sqrt(2.0 / math.pi)
GELU_CUBE = 0.044715


def gelu_pair(x):
    square = x * x
    t = jnp.tanh(GELU_SCALE * (x + GELU_CUBE * x * square))
    cdf = 0.5 * (1.0 + t)
    inner = GELU_SCALE * (1.0 + 3.0 * GELU_CUBE * square)
    return x * cdf, cdf + 0.5 * x * (1.0 - t * t) * inner


def rows_of(slot):
    return pl.ds(pl.multiple_of(slot * ROWS, ROWS), ROWS)


def over(first, last, body):
    def step(i, carry):
        body(i)
        return carry

    if first < last:
        lax.fori_loop(first, last, step, 0)


def remote(src, dst, send_sem, recv_sem, device):
    return pltpu.make_async_remote_copy(
        src_ref=src, dst_ref=dst, send_sem=send_sem, recv_sem=recv_sem,
        device_id=device, device_id_type=MESH)


class Line:
    def __init__(self, axis, n, place):
        self.n = n
        me = lax.axis_index(axis)
        self.pos = me // 2
        self.par = me % 2
        self.place = place

    def peer(self, pos):
        return self.place(pos * 2 + self.par)

    def other(self, pos):
        return self.place(pos * 2 + 1 - self.par)

    def at(self, i):
        j = (i + 1) // 2
        return lax.rem(self.pos + self.n // 2 + j * (1 - 2 * (i % 2)) + self.n, self.n)

    def peers(self, first, last, body):
        over(first, last, lambda i: body(self.at(i)))

    def peers_back(self, first, last, body):
        over(first, last, lambda i: body(self.at(first + last - 1 - i)))


class Gather:
    def __init__(self, line, buf, skip, far, ring_send, ring_recv, pair_send, pair_recv, far_send):
        self.line, self.buf, self.skip, self.far = line, buf, skip, far
        self.ring_send, self.ring_recv = ring_send, ring_recv
        self.pair_send, self.pair_recv = pair_send, pair_recv
        self.far_send = far_send

    def own(self, h):
        line = self.line
        return self.buf.at[h, rows_of(line.par * line.n + line.pos)]

    def ring(self, h, block_pos, peer_pos):
        line = self.line
        block = self.buf.at[h, rows_of(line.par * line.n + block_pos)]
        return remote(block, block, self.ring_send.at[h, peer_pos], self.ring_recv.at[h, block_pos], line.peer(peer_pos))

    def to_ring(self, h, pos):
        return self.ring(h, self.line.pos, pos)

    def from_ring(self, h, pos):
        return self.ring(h, pos, pos)

    def to_far(self, h, pos):
        line = self.line
        return remote(self.own(h), self.own(h), self.far_send.at[h, pos], self.pair_recv.at[h, line.pos], line.other(pos))

    def pair(self, h, par, pos):
        line = self.line
        block = self.buf.at[h, rows_of(par * line.n + pos)]
        return remote(block, block, self.pair_send.at[h, pos], self.pair_recv.at[h, pos], line.other(line.pos))

    def start(self, h):
        line = self.line

        def both(pos):
            self.to_ring(h, pos).start()
            self.to_far(h, pos).start()

        line.peers(self.skip, self.far, both)
        line.peers(max(self.skip, self.far), line.n - 1, lambda pos: self.to_ring(h, pos).start())
        self.pair(h, line.par, line.pos).start()

    def finish_ring(self, h):
        line = self.line

        def forward(pos):
            self.from_ring(h, pos).wait_recv()
            self.pair(h, line.par, pos).start()

        line.peers_back(self.far, line.n - 1, forward)
        line.peers_back(0, self.far, lambda pos: self.from_ring(h, pos).wait_recv())

    def finish_pair(self, h):
        line = self.line
        over(0, line.n, lambda pos: self.pair(h, 1 - line.par, pos).wait_recv())

    def drain(self, h):
        line = self.line
        line.peers(self.skip, line.n - 1, lambda pos: self.to_ring(h, pos).wait_send())
        line.peers(self.skip, self.far, lambda pos: self.to_far(h, pos).wait_send())
        line.peers(self.far, line.n - 1, lambda pos: self.pair(h, line.par, pos).wait_send())
        self.pair(h, line.par, line.pos).wait_send()


class Scatter:
    def __init__(self, line, far, whole, out, kept, got, both, land, far_land,
                 pair_send, pair_recv, ring_send, ring_recv, far_send, far_recv):
        self.line, self.far, self.whole = line, far, whole
        self.out, self.kept, self.got, self.both = out, kept, got, both
        self.land, self.far_land = land, far_land
        self.pair_send, self.pair_recv = pair_send, pair_recv
        self.ring_send, self.ring_recv = ring_send, ring_recv
        self.far_send, self.far_recv = far_send, far_recv

    def pair(self, h, pos):
        line = self.line
        if self.whole:
            return remote(self.out.at[h, 1 - line.par], self.got.at[h], self.pair_send.at[h, 0], self.pair_recv.at[h, 0], line.other(line.pos))
        return remote(self.out.at[h, 1 - line.par, rows_of(pos)], self.got.at[h, rows_of(pos)],
                      self.pair_send.at[h, pos], self.pair_recv.at[h, pos], line.other(line.pos))

    def ring(self, h, pos, land_pos):
        return remote(self.both.at[h, rows_of(pos)], self.land.at[h, rows_of(land_pos)],
                      self.ring_send.at[h, pos], self.ring_recv.at[h, land_pos], self.line.peer(pos))

    def to_ring(self, h, pos):
        return self.ring(h, pos, self.line.pos)

    def from_ring(self, h, pos):
        return self.ring(h, pos, pos)

    def direct(self, h, pos, land_pos):
        return remote(self.out.at[h, 1 - self.line.par, rows_of(pos)], self.far_land.at[h, rows_of(land_pos)],
                      self.far_send.at[h, pos], self.far_recv.at[h, land_pos], self.line.other(pos))

    def to_far(self, h, pos):
        return self.direct(h, pos, self.line.pos)

    def from_far(self, h, pos):
        return self.direct(h, pos, pos)

    def multiply(self, h, buf, w, transposed, par):
        size = self.line.n * ROWS
        width = w.shape[0]
        tile = min(TILE, width)
        left = buf[h, pl.ds(pl.multiple_of(par * size, size), size), :]

        def column(j):
            cut = pl.ds(pl.multiple_of(j * tile, tile), tile)
            if transposed:
                value = lax.dot_general(left, w[cut, :], (((1,), (1,)), ((), ())), preferred_element_type=jnp.float32)
            else:
                value = jnp.dot(left, w[:, cut], preferred_element_type=jnp.float32)
            self.kept[h, par, :, cut] = value
            self.out[h, par, :, cut] = value.astype(jnp.bfloat16)

        over(0, width // tile, column)

    def send_pair(self, h):
        line = self.line
        line.peers(0, self.far, lambda pos: self.to_far(h, pos).start())
        if not self.whole:
            line.peers(self.far, line.n - 1, lambda pos: self.pair(h, pos).start())
        self.pair(h, line.pos).start()

    def send_far(self, h):
        line = self.line

        def send(pos):
            self.both[h, rows_of(pos), :] = self.out[h, line.par, rows_of(pos), :]
            self.to_ring(h, pos).start()

        line.peers(0, self.far, send)

    def combine(self, h):
        line = self.line
        if self.whole:
            self.pair(h, 0).wait_recv()

        def send(pos):
            if not self.whole:
                self.pair(h, pos).wait_recv()
            total = self.kept[h, line.par, rows_of(pos), :] + self.got[h, rows_of(pos), :].astype(jnp.float32)
            self.both[h, rows_of(pos), :] = total.astype(jnp.bfloat16)
            self.to_ring(h, pos).start()

        line.peers(self.far, line.n - 1, send)

    def finish(self, h):
        line = self.line
        if not self.whole:
            self.pair(h, line.pos).wait_recv()
        total = self.kept[h, line.par, rows_of(line.pos), :] + self.got[h, rows_of(line.pos), :].astype(jnp.float32)

        def near(i, total):
            pos = line.at(line.n - 2 - i)
            self.from_ring(h, pos).wait_recv()
            return total + self.land[h, rows_of(pos), :].astype(jnp.float32)

        total = lax.fori_loop(0, line.n - 1, near, total)

        def far(i, total):
            pos = line.at(self.far - 1 - i)
            self.from_far(h, pos).wait_recv()
            return total + self.far_land[h, rows_of(pos), :].astype(jnp.float32)

        return lax.fori_loop(0, self.far, far, total) if self.far else total

    def drain(self, h):
        line = self.line
        if not self.whole:
            line.peers(self.far, line.n - 1, lambda pos: self.pair(h, pos).wait_send())
        self.pair(h, line.pos).wait_send()
        line.peers(0, line.n - 1, lambda pos: self.to_ring(h, pos).wait_send())
        line.peers(0, self.far, lambda pos: self.to_far(h, pos).wait_send())


def kernel(n, ends_hbm, w_hbm, routes_hbm, ends_out, dw_hbm,
           w, col_buf, row_buf, dy, outgoing, slope, route_row, route_tiles, dw,
           rs_out, rs_kept, rs_got, rs_both, rs_land, rs_far_land,
           ag_ring_send, ag_ring_recv, ag_pair_send, ag_pair_recv, ag_far_send,
           rs_ring_send, rs_ring_recv, rs_pair_send, rs_pair_recv, rs_far_send, rs_far_recv,
           cross_send, cross_recv, cross_far_send, slope_send, slope_recv,
           rt_send, rt_recv, rt_pair_send, rt_pair_recv, local_sem):
    s, r, c = lax.axis_index("section"), lax.axis_index("row"), lax.axis_index("col")
    row = Line("row", n, lambda i: (s, i, c))
    col = Line("col", n, lambda i: (s, r, i))
    over_there = (1 - s, r, c)
    far_gather, far_sum, far_cross = (min(far, n - 1) for far in (FAR_GATHER, FAR_SUM, FAR_CROSS))
    halves = range(HALVES)

    def gather(line, buf, skip, far, k):
        return Gather(line, buf, skip, far, ag_ring_send.at[k], ag_ring_recv.at[k],
                      ag_pair_send.at[k], ag_pair_recv.at[k], ag_far_send.at[k])

    ag_col = gather(col, col_buf, 0, far_gather, 0)
    ag_row = gather(row, row_buf, far_cross, 0, 1)

    def scatter(line, far, whole, k):
        return Scatter(line, far, whole, rs_out.at[k], rs_kept.at[k], rs_got.at[k], rs_both.at[k],
                       rs_land.at[k], rs_far_land, rs_pair_send.at[k], rs_pair_recv.at[k],
                       rs_ring_send.at[k], rs_ring_recv.at[k], rs_far_send, rs_far_recv)

    rs_row, rs_col = scatter(row, 0, WHOLE_ROW_PAIR, 0), scatter(col, far_sum, False, 1)

    def cross(h):
        return remote(outgoing.at[h], ag_row.own(h), cross_send.at[h], cross_recv.at[h], over_there)

    def cross_far(h, pos):
        return remote(outgoing.at[h], ag_row.own(h), cross_far_send.at[h, pos],
                      ag_row.ring_recv.at[h, row.pos], (1 - s, pos * 2 + row.par, c))

    def cross_slope(h):
        return remote(slope.at[h], slope.at[h], slope_send.at[h], slope_recv.at[h], over_there)

    def cross_start(h):
        cross(h).start()
        row.peers(0, far_cross, lambda pos: cross_far(h, pos).start())

    def cross_drain(h):
        cross(h).wait_send()
        row.peers(0, far_cross, lambda pos: cross_far(h, pos).wait_send())

    load_w = pltpu.make_async_copy(w_hbm.at[0], w, local_sem.at[0])
    store_dw = pltpu.make_async_copy(dw, dw_hbm.at[0], local_sem.at[1])
    load_routes = pltpu.make_async_copy(routes_hbm, route_row, local_sem.at[4])

    def load_ends(h, dst):
        return pltpu.make_async_copy(ends_hbm.at[0, pl.ds(h * ROWS, ROWS)], dst, local_sem.at[2 + h])

    barrier = pltpu.get_barrier_semaphore()

    def greet(device):
        pl.semaphore_signal(barrier, inc=1, device_id=device, device_id_type=MESH)

    far_col = max(far_gather, far_sum)
    col.peers(0, n - 1, lambda pos: greet(col.peer(pos)))
    col.peers(0, far_col, lambda pos: greet(col.other(pos)))
    greet(col.other(col.pos))
    row.peers(0, n - 1, lambda pos: greet(row.peer(pos)))
    greet(row.other(row.pos))
    greet(over_there)
    row.peers(0, far_cross, lambda pos: greet((1 - s, pos * 2 + row.par, c)))
    greetings = 2 * (n - 1) + 3 + far_col + far_cross

    def weight_grad():
        width = w.shape[0]
        tile = min(TILE, width)

        def block(k):
            at_row = pl.ds(pl.multiple_of((k // (width // tile)) * tile, tile), tile)
            at_col = pl.ds(pl.multiple_of((k % (width // tile)) * tile, tile), tile)
            total = jnp.zeros((tile, tile), jnp.float32)
            for h in halves:
                total = total + lax.dot_general(
                    col_buf[h, :, at_row], row_buf[h, :, at_col], (((0,), (0,)), ((), ())),
                    preferred_element_type=jnp.float32)
            dw[at_row, at_col] = total.astype(jnp.bfloat16)

        over(0, (width // tile) ** 2, block)
        store_dw.start()

    same = row.par == col.par
    differ = row.par != col.par

    def col_to_row():
        for h in halves:
            ag_col.finish_ring(h)
            if h == 0:
                pl.when(s == 0)(load_w.wait)
            rs_row.multiply(h, col_buf, w, False, col.par)
            pl.when(differ)(lambda: rs_row.send_pair(h))
            pl.when(same)(lambda: rs_row.combine(h))
        for h in halves:
            ag_col.finish_pair(h)
            rs_row.multiply(h, col_buf, w, False, 1 - col.par)
            pl.when(same)(lambda: rs_row.send_pair(h))
            pl.when(differ)(lambda: rs_row.combine(h))

    def row_to_col():
        for h in halves:
            ag_row.finish_ring(h)
            if h == 0:
                pl.when(s == 1)(load_w.wait)
            rs_col.multiply(h, row_buf, w, True, row.par)
            pl.when(differ)(lambda: rs_col.send_pair(h))
            pl.when(same)(lambda: rs_col.send_far(h))
            ag_row.finish_pair(h)
            rs_col.multiply(h, row_buf, w, True, 1 - row.par)
            pl.when(same)(lambda: rs_col.send_pair(h))
            pl.when(differ)(lambda: rs_col.send_far(h))
        for h in halves:
            rs_col.combine(h)

    @pl.when(s == 0)
    def _():
        for h in halves:
            load_ends(h, ag_col.own(h)).start()
        load_w.start()
        for h in halves:
            load_ends(h, ag_col.own(h)).wait()
        pl.semaphore_wait(barrier, greetings)
        for h in halves:
            ag_col.start(h)
        col_to_row()
        for h in halves:
            value, grad = gelu_pair(rs_row.finish(h))
            outgoing[h] = value.astype(jnp.bfloat16)
            cross_start(h)
            slope[h] = grad
            cross_slope(h).start()
        for h in halves:
            ag_col.drain(h)
            rs_row.drain(h)
            cross_drain(h)
            cross_slope(h).wait_send()
        for h in halves:
            cross(h).wait_recv()
            ag_row.start(h)
        row_to_col()
        weight_grad()
        for h in halves:
            ends_out[0, pl.ds(h * ROWS, ROWS), :] = rs_col.finish(h).astype(jnp.bfloat16)
        for h in halves:
            ag_row.drain(h)
            rs_col.drain(h)
        store_dw.wait()

    @pl.when(s == 1)
    def _():
        load_routes.start()
        for h in halves:
            load_ends(h, dy.at[h]).start()
        load_w.start()
        load_routes.wait()
        route_tiles[row.par, row.pos] = jnp.zeros((8, 128), jnp.float32)
        route_tiles[row.par, row.pos, 0:1, 0:2 * n] = route_row[...].astype(jnp.float32)
        for h in halves:
            load_ends(h, dy.at[h]).wait()
        pl.semaphore_wait(barrier, greetings)

        def tile_to(pos):
            mine = route_tiles.at[row.par, row.pos]
            return remote(mine, mine, rt_send.at[pos], rt_recv.at[row.pos], row.peer(pos))

        def tile_from(pos):
            tile = route_tiles.at[row.par, pos]
            return remote(tile, tile, rt_send.at[pos], rt_recv.at[pos], row.peer(pos))

        def tiles(par):
            return remote(route_tiles.at[par], route_tiles.at[par], rt_pair_send.at[0], rt_pair_recv.at[0], row.other(row.pos))

        row.peers(0, n - 1, lambda pos: tile_to(pos).start())
        row.peers(0, n - 1, lambda pos: tile_from(pos).wait_recv())
        tiles(row.par).start()
        tiles(1 - row.par).wait_recv()
        row.peers(0, n - 1, lambda pos: tile_to(pos).wait_send())
        tiles(row.par).wait_send()
        picked = route_tiles[col.par, col.pos, 0:1, :]
        lanes = lax.broadcasted_iota(jnp.int32, (1, 128), 1)
        routed = jnp.sum(jnp.where(lanes == r, picked, 0.0), axis=1, keepdims=True)

        for h in halves:
            cross(h).wait_recv()
            ag_row.start(h)
        row_to_col()
        for h in halves:
            value, grad = gelu_pair(rs_col.finish(h) * routed)
            masked = (dy[h].astype(jnp.float32) * grad).astype(jnp.bfloat16).astype(jnp.float32) * routed
            ag_col.own(h)[...] = masked.astype(jnp.bfloat16)
            ag_col.start(h)
            ends_out[0, pl.ds(h * ROWS, ROWS), :] = value.astype(jnp.bfloat16)
        col_to_row()
        for h in halves:
            grad_hidden = rs_row.finish(h).astype(jnp.bfloat16).astype(jnp.float32)
            cross_slope(h).wait_recv()
            outgoing[h] = (grad_hidden * slope[h]).astype(jnp.bfloat16)
            cross_start(h)
        weight_grad()
        for h in halves:
            ag_col.drain(h)
            rs_row.drain(h)
            ag_row.drain(h)
            rs_col.drain(h)
            cross_drain(h)
        store_dw.wait()


def shards(ends, weights, routes):
    width = weights.shape[1]
    n = lax.axis_size("row") // 2
    half = n * ROWS
    bf16, f32 = jnp.bfloat16, jnp.float32
    dma = pltpu.SemaphoreType.DMA
    anywhere = pl.BlockSpec(memory_space=pl.ANY)
    in_vmem = pl.BlockSpec(memory_space=pltpu.VMEM)
    lines = dma((2, HALVES, n))
    line = dma((HALVES, n))
    return pl.pallas_call(
        functools.partial(kernel, n),
        out_shape=(jax.ShapeDtypeStruct(ends.shape, bf16), jax.ShapeDtypeStruct(weights.shape, bf16)),
        in_specs=[anywhere, anywhere, anywhere],
        out_specs=(in_vmem, anywhere),
        scratch_shapes=[
            pltpu.VMEM((width, width), bf16),
            pltpu.VMEM((HALVES, 2 * half, width), bf16),
            pltpu.VMEM((HALVES, 2 * half, width), bf16),
            pltpu.VMEM((HALVES, ROWS, width), bf16),
            pltpu.VMEM((HALVES, ROWS, width), bf16),
            pltpu.VMEM((HALVES, ROWS, width), f32),
            pltpu.VMEM(routes.shape, jnp.int32),
            pltpu.VMEM((2, n, 8, 128), f32),
            pltpu.VMEM((width, width), bf16),
            pltpu.VMEM((2, HALVES, 2, half, width), bf16),
            pltpu.VMEM((2, HALVES, 2, half, width), f32),
            pltpu.VMEM((2, HALVES, half, width), bf16),
            pltpu.VMEM((2, HALVES, half, width), bf16),
            pltpu.VMEM((2, HALVES, half, width), bf16),
            pltpu.VMEM((HALVES, half, width), bf16),
            lines, lines, lines, lines, lines,
            lines, lines, lines, lines, line, line,
            dma((HALVES,)), dma((HALVES,)), line, dma((HALVES,)), dma((HALVES,)),
            dma((n,)), dma((n,)), dma((1,)), dma((1,)), dma((5,)),
        ],
        compiler_params=pltpu.CompilerParams(
            collective_id=0, has_side_effects=True, vmem_limit_bytes=VMEM_LIMIT),
        cost_estimate=pl.CostEstimate(
            flops=6 * half * 4 * width * width, bytes_accessed=4 * width * width, transcendentals=0),
    )(ends, weights, routes)


def solution(mesh):
    placed = (P("section", "col", "row"), P("section", "row", "col"), P("row", None))
    return jax.shard_map(
        shards,
        mesh=mesh,
        in_specs=placed,
        out_specs=(P("section", "col", "row"), P("section", "row", "col")),
        check_vma=False,
    )
```

```python
import functools
import math

import jax
import jax.numpy as jnp
from jax import lax
from jax.experimental import pallas as pl
from jax.experimental.pallas import tpu as pltpu
from jax.sharding import PartitionSpec as P

MESH = pl.DeviceIdType.MESH
PARTS = 2
ROWS = 16
LATE_COL = 1
LATE_ROW = 0
LATE_SUM = 1
TILE = 256
FAR_GATHER = 0
FAR_SUM = 0
FAR_CROSS = 0
WHOLE_ROW_PAIR = True
VMEM_LIMIT = 62 * 2**20
GELU_SCALE = math.sqrt(2.0 / math.pi)
GELU_CUBE = 0.044715


def gelu_pair(x):
    square = x * x
    t = jnp.tanh(GELU_SCALE * (x + GELU_CUBE * x * square))
    cdf = 0.5 * (1.0 + t)
    inner = GELU_SCALE * (1.0 + 3.0 * GELU_CUBE * square)
    return x * cdf, cdf + 0.5 * x * (1.0 - t * t) * inner


def over(first, last, body):
    def step(i, carry):
        body(i)
        return carry

    if first < last:
        lax.fori_loop(first, last, step, 0)


def remote(src, dst, send_sem, recv_sem, device):
    return pltpu.make_async_remote_copy(
        src_ref=src, dst_ref=dst, send_sem=send_sem, recv_sem=recv_sem,
        device_id=device, device_id_type=MESH)


class Line:
    def __init__(self, axis, n, place):
        self.n = n
        me = lax.axis_index(axis)
        self.pos = me // 2
        self.par = me % 2
        self.place = place

    def peer(self, pos):
        return self.place(pos * 2 + self.par)

    def other(self, pos):
        return self.place(pos * 2 + 1 - self.par)

    def at(self, i):
        j = (i + 1) // 2
        return lax.rem(self.pos + self.n // 2 + j * (1 - 2 * (i % 2)) + self.n, self.n)

    def peers(self, first, last, body):
        over(first, last, lambda i: body(self.at(i)))

    def peers_back(self, first, last, body):
        over(first, last, lambda i: body(self.at(first + last - 1 - i)))


class Gather:
    def __init__(self, line, buf, skip, far, ring_send, ring_recv, pair_send, pair_recv, far_send):
        self.line, self.buf, self.skip, self.far = line, buf, skip, far
        self.ring_send, self.ring_recv = ring_send, ring_recv
        self.pair_send, self.pair_recv = pair_send, pair_recv
        self.far_send = far_send

    def own(self, h):
        line = self.line
        return self.buf.at[h, line.par * line.n + line.pos]

    def ring(self, h, block_pos, peer_pos):
        line = self.line
        block = self.buf.at[h, line.par * line.n + block_pos]
        return remote(block, block, self.ring_send.at[h, peer_pos], self.ring_recv.at[h, block_pos], line.peer(peer_pos))

    def to_ring(self, h, pos):
        return self.ring(h, self.line.pos, pos)

    def from_ring(self, h, pos):
        return self.ring(h, pos, pos)

    def to_far(self, h, pos):
        line = self.line
        return remote(self.own(h), self.own(h), self.far_send.at[h, pos], self.pair_recv.at[h, line.pos], line.other(pos))

    def pair(self, h, par, pos):
        line = self.line
        block = self.buf.at[h, par * line.n + pos]
        return remote(block, block, self.pair_send.at[h, pos], self.pair_recv.at[h, pos], line.other(line.pos))

    def start(self, h):
        line = self.line

        def both(pos):
            self.to_ring(h, pos).start()
            self.to_far(h, pos).start()

        line.peers(self.skip, self.far, both)
        line.peers(max(self.skip, self.far), line.n - 1, lambda pos: self.to_ring(h, pos).start())
        self.pair(h, line.par, line.pos).start()

    def finish_ring(self, h):
        line = self.line

        def forward(pos):
            self.from_ring(h, pos).wait_recv()
            self.pair(h, line.par, pos).start()

        line.peers_back(self.far, line.n - 1, forward)
        line.peers_back(0, self.far, lambda pos: self.from_ring(h, pos).wait_recv())

    def finish_pair(self, h):
        line = self.line
        over(0, line.n, lambda pos: self.pair(h, 1 - line.par, pos).wait_recv())

    def drain(self, h):
        line = self.line
        line.peers(self.skip, line.n - 1, lambda pos: self.to_ring(h, pos).wait_send())
        line.peers(self.skip, self.far, lambda pos: self.to_far(h, pos).wait_send())
        line.peers(self.far, line.n - 1, lambda pos: self.pair(h, line.par, pos).wait_send())
        self.pair(h, line.par, line.pos).wait_send()


class Scatter:
    def __init__(self, line, far, whole, out, kept, got, both, land, far_land,
                 pair_send, pair_recv, ring_send, ring_recv, far_send, far_recv):
        self.line, self.far, self.whole = line, far, whole
        self.out, self.kept, self.got, self.both = out, kept, got, both
        self.land, self.far_land = land, far_land
        self.pair_send, self.pair_recv = pair_send, pair_recv
        self.ring_send, self.ring_recv = ring_send, ring_recv
        self.far_send, self.far_recv = far_send, far_recv

    def pair(self, h, pos):
        line = self.line
        if self.whole:
            return remote(self.out.at[h, 1 - line.par], self.got.at[h], self.pair_send.at[h, 0], self.pair_recv.at[h, 0], line.other(line.pos))
        return remote(self.out.at[h, 1 - line.par, pos], self.got.at[h, pos],
                      self.pair_send.at[h, pos], self.pair_recv.at[h, pos], line.other(line.pos))

    def ring(self, h, pos, land_pos):
        return remote(self.both.at[h, pos], self.land.at[h, land_pos],
                      self.ring_send.at[h, pos], self.ring_recv.at[h, land_pos], self.line.peer(pos))

    def to_ring(self, h, pos):
        return self.ring(h, pos, self.line.pos)

    def from_ring(self, h, pos):
        return self.ring(h, pos, pos)

    def direct(self, h, pos, land_pos):
        return remote(self.out.at[h, 1 - self.line.par, pos], self.far_land.at[h, land_pos],
                      self.far_send.at[h, pos], self.far_recv.at[h, land_pos], self.line.other(pos))

    def to_far(self, h, pos):
        return self.direct(h, pos, self.line.pos)

    def from_far(self, h, pos):
        return self.direct(h, pos, pos)

    def multiply(self, h, buf, w, transposed, par):
        n = self.line.n
        width = w.shape[0]
        tile = min(TILE, width)
        left = buf[h, pl.ds(par * n, n)].reshape(n * ROWS, width)

        def column(j):
            cut = pl.ds(j * tile, tile)
            if transposed:
                value = lax.dot_general(left, w[cut, :], (((1,), (1,)), ((), ())), preferred_element_type=jnp.float32)
            else:
                value = jnp.dot(left, w[:, cut], preferred_element_type=jnp.float32)
            self.kept[h, par, :, :, cut] = value.reshape(n, ROWS, tile)
            self.out[h, par, :, :, cut] = value.astype(jnp.bfloat16).reshape(n, ROWS, tile)

        for j in range(width // tile):
            column(j)

    def send_pair(self, h):
        line = self.line
        line.peers(0, self.far, lambda pos: self.to_far(h, pos).start())
        if not self.whole:
            line.peers(self.far, line.n - 1, lambda pos: self.pair(h, pos).start())
        self.pair(h, line.pos).start()

    def send_far(self, h):
        line = self.line

        def send(pos):
            self.both[h, pos, :] = self.out[h, line.par, pos, :]
            self.to_ring(h, pos).start()

        line.peers(0, self.far, send)

    def combine(self, h):
        line = self.line
        if self.whole:
            self.pair(h, 0).wait_recv()

        def send(pos):
            if not self.whole:
                self.pair(h, pos).wait_recv()
            total = self.kept[h, line.par, pos, :] + self.got[h, pos, :].astype(jnp.float32)
            self.both[h, pos, :] = total.astype(jnp.bfloat16)
            self.to_ring(h, pos).start()

        line.peers(self.far, line.n - 1, send)

    def finish(self, h):
        line = self.line
        if not self.whole:
            self.pair(h, line.pos).wait_recv()
        total = self.kept[h, line.par, line.pos, :] + self.got[h, line.pos, :].astype(jnp.float32)

        def near(i, total):
            pos = line.at(line.n - 2 - i)
            self.from_ring(h, pos).wait_recv()
            return total + self.land[h, pos, :].astype(jnp.float32)

        total = lax.fori_loop(0, line.n - 1, near, total)

        def far(i, total):
            pos = line.at(self.far - 1 - i)
            self.from_far(h, pos).wait_recv()
            return total + self.far_land[h, pos, :].astype(jnp.float32)

        return lax.fori_loop(0, self.far, far, total) if self.far else total

    def drain(self, h):
        line = self.line
        if not self.whole:
            line.peers(self.far, line.n - 1, lambda pos: self.pair(h, pos).wait_send())
        self.pair(h, line.pos).wait_send()
        line.peers(0, line.n - 1, lambda pos: self.to_ring(h, pos).wait_send())
        line.peers(0, self.far, lambda pos: self.to_far(h, pos).wait_send())


def kernel(n, ends_hbm, w_hbm, routes_hbm, ends_out, dw_hbm,
           w, ends, col_buf, row_buf, outgoing, slope, route_row, route_tiles, dw,
           rs_out, rs_kept, rs_got, rs_both, rs_land, rs_far_land,
           ag_ring_send, ag_ring_recv, ag_pair_send, ag_pair_recv, ag_far_send,
           rs_ring_send, rs_ring_recv, rs_pair_send, rs_pair_recv, rs_far_send, rs_far_recv,
           cross_send, cross_recv, cross_far_send, slope_send, slope_recv,
           rt_send, rt_recv, rt_pair_send, rt_pair_recv, local_sem):
    s, r, c = lax.axis_index("section"), lax.axis_index("row"), lax.axis_index("col")
    row = Line("row", n, lambda i: (s, i, c))
    col = Line("col", n, lambda i: (s, r, i))
    over_there = (1 - s, r, c)
    far_gather, far_sum, far_cross = (min(far, n - 1) for far in (FAR_GATHER, FAR_SUM, FAR_CROSS))
    parts = range(PARTS)

    def gather(line, buf, skip, far, k):
        return Gather(line, buf, skip, far, ag_ring_send.at[k], ag_ring_recv.at[k],
                      ag_pair_send.at[k], ag_pair_recv.at[k], ag_far_send.at[k])

    ag_col = gather(col, col_buf, 0, far_gather, 0)
    ag_row = gather(row, row_buf, far_cross, 0, 1)

    def scatter(line, far, whole, k):
        return Scatter(line, far, whole, rs_out.at[k], rs_kept.at[k], rs_got.at[k], rs_both.at[k],
                       rs_land.at[k], rs_far_land, rs_pair_send.at[k], rs_pair_recv.at[k],
                       rs_ring_send.at[k], rs_ring_recv.at[k], rs_far_send, rs_far_recv)

    rs_row, rs_col = scatter(row, 0, WHOLE_ROW_PAIR, 0), scatter(col, far_sum, False, 1)

    def cross(h):
        return remote(outgoing.at[h], ag_row.own(h), cross_send.at[h], cross_recv.at[h], over_there)

    def cross_far(h, pos):
        return remote(outgoing.at[h], ag_row.own(h), cross_far_send.at[h, pos],
                      ag_row.ring_recv.at[h, row.pos], (1 - s, pos * 2 + row.par, c))

    def cross_slope(h):
        return remote(slope.at[h], slope.at[h], slope_send.at[h], slope_recv.at[h], over_there)

    def cross_start(h):
        cross(h).start()
        row.peers(0, far_cross, lambda pos: cross_far(h, pos).start())

    def cross_drain(h):
        cross(h).wait_send()
        row.peers(0, far_cross, lambda pos: cross_far(h, pos).wait_send())

    load_w = pltpu.make_async_copy(w_hbm.at[0], w, local_sem.at[0])
    store_dw = pltpu.make_async_copy(dw, dw_hbm.at[0], local_sem.at[1])
    load_routes = pltpu.make_async_copy(routes_hbm, route_row, local_sem.at[3])

    load_ends = pltpu.make_async_copy(ends_hbm.at[0], ends, local_sem.at[2])

    def ends_part(h):
        return ends[pl.ds(h * ROWS, ROWS), :]

    barrier = pltpu.get_barrier_semaphore()

    def greet(device):
        pl.semaphore_signal(barrier, inc=1, device_id=device, device_id_type=MESH)

    far_col = max(far_gather, far_sum)
    col.peers(0, n - 1, lambda pos: greet(col.peer(pos)))
    col.peers(0, far_col, lambda pos: greet(col.other(pos)))
    greet(col.other(col.pos))
    row.peers(0, n - 1, lambda pos: greet(row.peer(pos)))
    greet(row.other(row.pos))
    greet(over_there)
    row.peers(0, far_cross, lambda pos: greet((1 - s, pos * 2 + row.par, c)))
    greetings = 2 * (n - 1) + 3 + far_col + far_cross

    def weight_grad():
        width = w.shape[0]
        tile = min(TILE, width)

        def block(k):
            at_row = pl.ds(pl.multiple_of((k // (width // tile)) * tile, tile), tile)
            at_col = pl.ds(pl.multiple_of((k % (width // tile)) * tile, tile), tile)
            total = jnp.zeros((tile, tile), jnp.float32)
            for h in parts:
                total = total + lax.dot_general(
                    col_buf[h, :, :, at_row].reshape(-1, tile), row_buf[h, :, :, at_col].reshape(-1, tile),
                    (((0,), (0,)), ((), ())),
                    preferred_element_type=jnp.float32)
            dw[at_row, at_col] = total.astype(jnp.bfloat16)

        over(0, (width // tile) ** 2, block)
        store_dw.start()

    same = row.par == col.par
    differ = row.par != col.par

    def staggered(early, late, lag):
        for h in range(PARTS + lag):
            if h < PARTS:
                early(h)
            if h >= lag:
                late(h - lag)

    def col_to_row():
        def early(h):
            ag_col.finish_ring(h)
            if h == 0:
                pl.when(s == 0)(load_w.wait)
            rs_row.multiply(h, col_buf, w, False, col.par)
            pl.when(differ)(lambda: rs_row.send_pair(h))
            pl.when(same)(lambda: rs_row.combine(h))

        def late(h):
            ag_col.finish_pair(h)
            rs_row.multiply(h, col_buf, w, False, 1 - col.par)
            pl.when(same)(lambda: rs_row.send_pair(h))
            pl.when(differ)(lambda: rs_row.combine(h))

        staggered(early, late, LATE_COL)

    def row_to_col():
        def early(h):
            ag_row.finish_ring(h)
            if h == 0:
                pl.when(s == 1)(load_w.wait)
            rs_col.multiply(h, row_buf, w, True, row.par)
            pl.when(differ)(lambda: rs_col.send_pair(h))
            pl.when(same)(lambda: rs_col.send_far(h))

        def late(h):
            ag_row.finish_pair(h)
            rs_col.multiply(h, row_buf, w, True, 1 - row.par)
            pl.when(same)(lambda: rs_col.send_pair(h))
            pl.when(differ)(lambda: rs_col.send_far(h))

        for h in range(PARTS + max(LATE_ROW, LATE_SUM)):
            if h < PARTS:
                early(h)
            if 0 <= h - LATE_SUM < PARTS:
                rs_col.combine(h - LATE_SUM)
            if 0 <= h - LATE_ROW < PARTS:
                late(h - LATE_ROW)

    @pl.when(s == 0)
    def _():
        load_ends.start()
        load_w.start()
        load_ends.wait()
        for h in parts:
            ag_col.own(h)[...] = ends_part(h)
        pl.semaphore_wait(barrier, greetings)
        for h in parts:
            ag_col.start(h)
        col_to_row()
        for h in parts:
            value, grad = gelu_pair(rs_row.finish(h))
            outgoing[h] = value.astype(jnp.bfloat16)
            cross_start(h)
            slope[h] = grad
            cross_slope(h).start()
        for h in parts:
            ag_col.drain(h)
            rs_row.drain(h)
            cross_drain(h)
            cross_slope(h).wait_send()
        for h in parts:
            cross(h).wait_recv()
            ag_row.start(h)
        row_to_col()
        weight_grad()
        for h in parts:
            ends_out[0, pl.ds(h * ROWS, ROWS), :] = rs_col.finish(h).astype(jnp.bfloat16)
        for h in parts:
            ag_row.drain(h)
            rs_col.drain(h)
        store_dw.wait()

    @pl.when(s == 1)
    def _():
        load_routes.start()
        load_ends.start()
        load_w.start()
        load_routes.wait()
        route_tiles[row.par, row.pos] = jnp.zeros((8, 128), jnp.float32)
        route_tiles[row.par, row.pos, 0:1, 0:2 * n] = route_row[...].astype(jnp.float32)
        load_ends.wait()
        pl.semaphore_wait(barrier, greetings)

        def tile_to(pos):
            mine = route_tiles.at[row.par, row.pos]
            return remote(mine, mine, rt_send.at[pos], rt_recv.at[row.pos], row.peer(pos))

        def tile_from(pos):
            tile = route_tiles.at[row.par, pos]
            return remote(tile, tile, rt_send.at[pos], rt_recv.at[pos], row.peer(pos))

        def tiles(par):
            return remote(route_tiles.at[par], route_tiles.at[par], rt_pair_send.at[0], rt_pair_recv.at[0], row.other(row.pos))

        row.peers(0, n - 1, lambda pos: tile_to(pos).start())
        row.peers(0, n - 1, lambda pos: tile_from(pos).wait_recv())
        tiles(row.par).start()
        tiles(1 - row.par).wait_recv()
        row.peers(0, n - 1, lambda pos: tile_to(pos).wait_send())
        tiles(row.par).wait_send()
        picked = route_tiles[col.par, col.pos, 0:1, :]
        lanes = lax.broadcasted_iota(jnp.int32, (1, 128), 1)
        routed = jnp.sum(jnp.where(lanes == r, picked, 0.0), axis=1, keepdims=True)

        for h in parts:
            cross(h).wait_recv()
            ag_row.start(h)
        row_to_col()
        for h in parts:
            value, grad = gelu_pair(rs_col.finish(h) * routed)
            masked = (ends_part(h).astype(jnp.float32) * grad).astype(jnp.bfloat16).astype(jnp.float32) * routed
            ag_col.own(h)[...] = masked.astype(jnp.bfloat16)
            ag_col.start(h)
            ends_out[0, pl.ds(h * ROWS, ROWS), :] = value.astype(jnp.bfloat16)
        col_to_row()
        for h in parts:
            grad_hidden = rs_row.finish(h).astype(jnp.bfloat16).astype(jnp.float32)
            cross_slope(h).wait_recv()
            outgoing[h] = (grad_hidden * slope[h]).astype(jnp.bfloat16)
            cross_start(h)
        weight_grad()
        for h in parts:
            ag_col.drain(h)
            rs_row.drain(h)
            ag_row.drain(h)
            rs_col.drain(h)
            cross_drain(h)
        store_dw.wait()


def shards(ends, weights, routes):
    width = weights.shape[1]
    n = lax.axis_size("row") // 2
    bf16, f32 = jnp.bfloat16, jnp.float32
    dma = pltpu.SemaphoreType.DMA
    anywhere = pl.BlockSpec(memory_space=pl.ANY)
    in_vmem = pl.BlockSpec(memory_space=pltpu.VMEM)
    lines = dma((2, PARTS, n))
    line = dma((PARTS, n))
    return pl.pallas_call(
        functools.partial(kernel, n),
        out_shape=(jax.ShapeDtypeStruct(ends.shape, bf16), jax.ShapeDtypeStruct(weights.shape, bf16)),
        in_specs=[anywhere, anywhere, anywhere],
        out_specs=(in_vmem, anywhere),
        scratch_shapes=[
            pltpu.VMEM((width, width), bf16),
            pltpu.VMEM(ends.shape[1:], bf16),
            pltpu.VMEM((PARTS, 2 * n, ROWS, width), bf16),
            pltpu.VMEM((PARTS, 2 * n, ROWS, width), bf16),
            pltpu.VMEM((PARTS, ROWS, width), bf16),
            pltpu.VMEM((PARTS, ROWS, width), f32),
            pltpu.VMEM(routes.shape, jnp.int32),
            pltpu.VMEM((2, n, 8, 128), f32),
            pltpu.VMEM((width, width), bf16),
            pltpu.VMEM((2, PARTS, 2, n, ROWS, width), bf16),
            pltpu.VMEM((2, PARTS, 2, n, ROWS, width), f32),
            pltpu.VMEM((2, PARTS, n, ROWS, width), bf16),
            pltpu.VMEM((2, PARTS, n, ROWS, width), bf16),
            pltpu.VMEM((2, PARTS, n, ROWS, width), bf16),
            pltpu.VMEM((PARTS, n, ROWS, width), bf16),
            lines, lines, lines, lines, lines,
            lines, lines, lines, lines, line, line,
            dma((PARTS,)), dma((PARTS,)), line, dma((PARTS,)), dma((PARTS,)),
            dma((n,)), dma((n,)), dma((1,)), dma((1,)), dma((4,)),
        ],
        compiler_params=pltpu.CompilerParams(
            collective_id=0, has_side_effects=True, vmem_limit_bytes=VMEM_LIMIT),
        cost_estimate=pl.CostEstimate(
            flops=24 * n * PARTS * ROWS * width * width, bytes_accessed=4 * width * width, transcendentals=0),
    )(ends, weights, routes)


def solution(mesh):
    placed = (P("section", "col", "row"), P("section", "row", "col"), P("row", None))
    return jax.shard_map(
        shards,
        mesh=mesh,
        in_specs=placed,
        out_specs=(P("section", "col", "row"), P("section", "row", "col")),
        check_vma=False,
    )
```

```python
import functools
import math

import jax
import jax.numpy as jnp
from jax import lax
from jax.experimental import pallas as pl
from jax.experimental.pallas import tpu as pltpu
from jax.sharding import PartitionSpec as P

MESH = pl.DeviceIdType.MESH
PARTS = 2
ROWS = 16
LATE_COL = 1
LATE_ROW = 0
LATE_SUM = 1
TILE = 256
FAR_GATHER = 0
FAR_SUM = 0
FAR_CROSS = 0
WHOLE_ROW_PAIR = True
VMEM_LIMIT = 62 * 2**20
GELU_SCALE = math.sqrt(2.0 / math.pi)
GELU_CUBE = 0.044715


def gelu_pair(x):
    square = x * x
    t = jnp.tanh(GELU_SCALE * (x + GELU_CUBE * x * square))
    cdf = 0.5 * (1.0 + t)
    inner = GELU_SCALE * (1.0 + 3.0 * GELU_CUBE * square)
    return x * cdf, cdf + 0.5 * x * (1.0 - t * t) * inner


def over(first, last, body):
    def step(i, carry):
        body(i)
        return carry

    if first < last:
        lax.fori_loop(first, last, step, 0, unroll=last - first < 9)


def remote(src, dst, send_sem, recv_sem, device):
    return pltpu.make_async_remote_copy(
        src_ref=src, dst_ref=dst, send_sem=send_sem, recv_sem=recv_sem,
        device_id=device, device_id_type=MESH)


class Line:
    def __init__(self, axis, n, place):
        self.n = n
        me = lax.axis_index(axis)
        self.pos = me // 2
        self.par = me % 2
        self.place = place

    def peer(self, pos):
        return self.place(pos * 2 + self.par)

    def other(self, pos):
        return self.place(pos * 2 + 1 - self.par)

    def at(self, i):
        j = (i + 1) // 2
        return lax.rem(self.pos + self.n // 2 + j * (1 - 2 * (i % 2)) + self.n, self.n)

    def peers(self, first, last, body):
        over(first, last, lambda i: body(self.at(i)))

    def peers_back(self, first, last, body):
        over(first, last, lambda i: body(self.at(first + last - 1 - i)))


class Gather:
    def __init__(self, line, buf, skip, far, ring_send, ring_recv, pair_send, pair_recv, far_send):
        self.line, self.buf, self.skip, self.far = line, buf, skip, far
        self.ring_send, self.ring_recv = ring_send, ring_recv
        self.pair_send, self.pair_recv = pair_send, pair_recv
        self.far_send = far_send

    def own(self, h):
        line = self.line
        return self.buf.at[h, line.par * line.n + line.pos]

    def ring(self, h, block_pos, peer_pos):
        line = self.line
        block = self.buf.at[h, line.par * line.n + block_pos]
        return remote(block, block, self.ring_send.at[h, peer_pos], self.ring_recv.at[h, block_pos], line.peer(peer_pos))

    def to_ring(self, h, pos):
        return self.ring(h, self.line.pos, pos)

    def from_ring(self, h, pos):
        return self.ring(h, pos, pos)

    def to_far(self, h, pos):
        line = self.line
        return remote(self.own(h), self.own(h), self.far_send.at[h, pos], self.pair_recv.at[h, line.pos], line.other(pos))

    def pair(self, h, par, pos):
        line = self.line
        block = self.buf.at[h, par * line.n + pos]
        return remote(block, block, self.pair_send.at[h, pos], self.pair_recv.at[h, pos], line.other(line.pos))

    def start(self, h):
        line = self.line

        def both(pos):
            self.to_ring(h, pos).start()
            self.to_far(h, pos).start()

        line.peers(self.skip, self.far, both)
        line.peers(max(self.skip, self.far), line.n - 1, lambda pos: self.to_ring(h, pos).start())
        self.pair(h, line.par, line.pos).start()

    def finish_ring(self, h):
        line = self.line

        def forward(pos):
            self.from_ring(h, pos).wait_recv()
            self.pair(h, line.par, pos).start()

        line.peers_back(self.far, line.n - 1, forward)
        line.peers_back(0, self.far, lambda pos: self.from_ring(h, pos).wait_recv())

    def finish_pair(self, h):
        line = self.line
        over(0, line.n, lambda pos: self.pair(h, 1 - line.par, pos).wait_recv())

    def drain(self, h):
        line = self.line
        line.peers(self.skip, line.n - 1, lambda pos: self.to_ring(h, pos).wait_send())
        line.peers(self.skip, self.far, lambda pos: self.to_far(h, pos).wait_send())
        line.peers(self.far, line.n - 1, lambda pos: self.pair(h, line.par, pos).wait_send())
        self.pair(h, line.par, line.pos).wait_send()


class Scatter:
    def __init__(self, line, far, whole, out, kept, got, both, land, far_land,
                 pair_send, pair_recv, ring_send, ring_recv, far_send, far_recv):
        self.line, self.far, self.whole = line, far, whole
        self.out, self.kept, self.got, self.both = out, kept, got, both
        self.land, self.far_land = land, far_land
        self.pair_send, self.pair_recv = pair_send, pair_recv
        self.ring_send, self.ring_recv = ring_send, ring_recv
        self.far_send, self.far_recv = far_send, far_recv

    def pair(self, h, pos):
        line = self.line
        if self.whole:
            return remote(self.out.at[h, 1 - line.par], self.got.at[h], self.pair_send.at[h, 0], self.pair_recv.at[h, 0], line.other(line.pos))
        return remote(self.out.at[h, 1 - line.par, pos], self.got.at[h, pos],
                      self.pair_send.at[h, pos], self.pair_recv.at[h, pos], line.other(line.pos))

    def ring(self, h, pos, land_pos):
        return remote(self.both.at[h, pos], self.land.at[h, land_pos],
                      self.ring_send.at[h, pos], self.ring_recv.at[h, land_pos], self.line.peer(pos))

    def to_ring(self, h, pos):
        return self.ring(h, pos, self.line.pos)

    def from_ring(self, h, pos):
        return self.ring(h, pos, pos)

    def direct(self, h, pos, land_pos):
        return remote(self.out.at[h, 1 - self.line.par, pos], self.far_land.at[h, land_pos],
                      self.far_send.at[h, pos], self.far_recv.at[h, land_pos], self.line.other(pos))

    def to_far(self, h, pos):
        return self.direct(h, pos, self.line.pos)

    def from_far(self, h, pos):
        return self.direct(h, pos, pos)

    def multiply(self, h, buf, w, transposed, par):
        n = self.line.n
        width = w.shape[0]
        tile = min(TILE, width)
        left = buf[h, pl.ds(par * n, n)].reshape(n * ROWS, width)

        def column(j):
            cut = pl.ds(j * tile, tile)
            if transposed:
                value = lax.dot_general(left, w[cut, :], (((1,), (1,)), ((), ())), preferred_element_type=jnp.float32)
            else:
                value = jnp.dot(left, w[:, cut], preferred_element_type=jnp.float32)
            self.kept[h, par, :, :, cut] = value.reshape(n, ROWS, tile)
            self.out[h, par, :, :, cut] = value.astype(jnp.bfloat16).reshape(n, ROWS, tile)

        for j in range(width // tile):
            column(j)

    def send_pair(self, h):
        line = self.line
        line.peers(0, self.far, lambda pos: self.to_far(h, pos).start())
        if not self.whole:
            line.peers(self.far, line.n - 1, lambda pos: self.pair(h, pos).start())
        self.pair(h, line.pos).start()

    def send_far(self, h):
        line = self.line

        def send(pos):
            self.both[h, pos, :] = self.out[h, line.par, pos, :]
            self.to_ring(h, pos).start()

        line.peers(0, self.far, send)

    def combine(self, h):
        line = self.line
        if self.whole:
            self.pair(h, 0).wait_recv()

        def send(pos):
            if not self.whole:
                self.pair(h, pos).wait_recv()
            total = self.kept[h, line.par, pos, :] + self.got[h, pos, :].astype(jnp.float32)
            self.both[h, pos, :] = total.astype(jnp.bfloat16)
            self.to_ring(h, pos).start()

        line.peers(self.far, line.n - 1, send)

    def finish(self, h):
        line = self.line
        if not self.whole:
            self.pair(h, line.pos).wait_recv()
        total = self.kept[h, line.par, line.pos, :] + self.got[h, line.pos, :].astype(jnp.float32)

        def near(i, total):
            pos = line.at(line.n - 2 - i)
            self.from_ring(h, pos).wait_recv()
            return total + self.land[h, pos, :].astype(jnp.float32)

        total = lax.fori_loop(0, line.n - 1, near, total, unroll=True)

        def far(i, total):
            pos = line.at(self.far - 1 - i)
            self.from_far(h, pos).wait_recv()
            return total + self.far_land[h, pos, :].astype(jnp.float32)

        return lax.fori_loop(0, self.far, far, total) if self.far else total

    def drain(self, h):
        line = self.line
        if not self.whole:
            line.peers(self.far, line.n - 1, lambda pos: self.pair(h, pos).wait_send())
        self.pair(h, line.pos).wait_send()
        line.peers(0, line.n - 1, lambda pos: self.to_ring(h, pos).wait_send())
        line.peers(0, self.far, lambda pos: self.to_far(h, pos).wait_send())


def kernel(n, ends_hbm, w_hbm, routes_hbm, ends_out, dw_hbm,
           w, ends, col_buf, row_buf, outgoing, slope, route_row, route_tiles, dw,
           rs_out, rs_kept, rs_got, rs_both, rs_land, rs_far_land,
           ag_ring_send, ag_ring_recv, ag_pair_send, ag_pair_recv, ag_far_send,
           rs_ring_send, rs_ring_recv, rs_pair_send, rs_pair_recv, rs_far_send, rs_far_recv,
           cross_send, cross_recv, cross_far_send, slope_send, slope_recv,
           rt_send, rt_recv, rt_pair_send, rt_pair_recv, local_sem):
    s, r, c = lax.axis_index("section"), lax.axis_index("row"), lax.axis_index("col")
    row = Line("row", n, lambda i: (s, i, c))
    col = Line("col", n, lambda i: (s, r, i))
    over_there = (1 - s, r, c)
    far_gather, far_sum, far_cross = (min(far, n - 1) for far in (FAR_GATHER, FAR_SUM, FAR_CROSS))
    parts = range(PARTS)

    def gather(line, buf, skip, far, k):
        return Gather(line, buf, skip, far, ag_ring_send.at[k], ag_ring_recv.at[k],
                      ag_pair_send.at[k], ag_pair_recv.at[k], ag_far_send.at[k])

    ag_col = gather(col, col_buf, 0, far_gather, 0)
    ag_row = gather(row, row_buf, far_cross, 0, 1)

    def scatter(line, far, whole, k):
        return Scatter(line, far, whole, rs_out.at[k], rs_kept.at[k], rs_got.at[k], rs_both.at[k],
                       rs_land.at[k], rs_far_land, rs_pair_send.at[k], rs_pair_recv.at[k],
                       rs_ring_send.at[k], rs_ring_recv.at[k], rs_far_send, rs_far_recv)

    rs_row, rs_col = scatter(row, 0, WHOLE_ROW_PAIR, 0), scatter(col, far_sum, False, 1)

    def cross(h):
        return remote(outgoing.at[h], ag_row.own(h), cross_send.at[h], cross_recv.at[h], over_there)

    def cross_far(h, pos):
        return remote(outgoing.at[h], ag_row.own(h), cross_far_send.at[h, pos],
                      ag_row.ring_recv.at[h, row.pos], (1 - s, pos * 2 + row.par, c))

    def cross_slope(h):
        return remote(slope.at[h], slope.at[h], slope_send.at[h], slope_recv.at[h], over_there)

    def cross_start(h):
        cross(h).start()
        row.peers(0, far_cross, lambda pos: cross_far(h, pos).start())

    def cross_drain(h):
        cross(h).wait_send()
        row.peers(0, far_cross, lambda pos: cross_far(h, pos).wait_send())

    load_w = pltpu.make_async_copy(w_hbm.at[0], w, local_sem.at[0])
    store_dw = pltpu.make_async_copy(dw, dw_hbm.at[0], local_sem.at[1])
    load_routes = pltpu.make_async_copy(routes_hbm, route_row, local_sem.at[3])

    load_ends = pltpu.make_async_copy(ends_hbm.at[0], ends, local_sem.at[2])

    def ends_part(h):
        return ends[pl.ds(h * ROWS, ROWS), :]

    barrier = pltpu.get_barrier_semaphore()

    def greet(device):
        pl.semaphore_signal(barrier, inc=1, device_id=device, device_id_type=MESH)

    far_col = max(far_gather, far_sum)
    col.peers(0, n - 1, lambda pos: greet(col.peer(pos)))
    col.peers(0, far_col, lambda pos: greet(col.other(pos)))
    greet(col.other(col.pos))
    row.peers(0, n - 1, lambda pos: greet(row.peer(pos)))
    greet(row.other(row.pos))
    greet(over_there)
    row.peers(0, far_cross, lambda pos: greet((1 - s, pos * 2 + row.par, c)))
    greetings = 2 * (n - 1) + 3 + far_col + far_cross

    def weight_grad():
        width = w.shape[0]
        tile = min(TILE, width)

        def block(k):
            at_row = pl.ds(pl.multiple_of((k // (width // tile)) * tile, tile), tile)
            at_col = pl.ds(pl.multiple_of((k % (width // tile)) * tile, tile), tile)
            total = jnp.zeros((tile, tile), jnp.float32)
            for h in parts:
                total = total + lax.dot_general(
                    col_buf[h, :, :, at_row].reshape(-1, tile), row_buf[h, :, :, at_col].reshape(-1, tile),
                    (((0,), (0,)), ((), ())),
                    preferred_element_type=jnp.float32)
            dw[at_row, at_col] = total.astype(jnp.bfloat16)

        over(0, (width // tile) ** 2, block)
        store_dw.start()

    same = row.par == col.par
    differ = row.par != col.par

    def staggered(early, late, lag):
        for h in range(PARTS + lag):
            if h < PARTS:
                early(h)
            if h >= lag:
                late(h - lag)

    def col_to_row():
        def early(h):
            ag_col.finish_ring(h)
            if h == 0:
                pl.when(s == 0)(load_w.wait)
            rs_row.multiply(h, col_buf, w, False, col.par)
            pl.when(differ)(lambda: rs_row.send_pair(h))
            pl.when(same)(lambda: rs_row.combine(h))

        def late(h):
            ag_col.finish_pair(h)
            rs_row.multiply(h, col_buf, w, False, 1 - col.par)
            pl.when(same)(lambda: rs_row.send_pair(h))
            pl.when(differ)(lambda: rs_row.combine(h))

        staggered(early, late, LATE_COL)

    def row_to_col():
        def early(h):
            ag_row.finish_ring(h)
            if h == 0:
                pl.when(s == 1)(load_w.wait)
            rs_col.multiply(h, row_buf, w, True, row.par)
            pl.when(differ)(lambda: rs_col.send_pair(h))
            pl.when(same)(lambda: rs_col.send_far(h))

        def late(h):
            ag_row.finish_pair(h)
            rs_col.multiply(h, row_buf, w, True, 1 - row.par)
            pl.when(same)(lambda: rs_col.send_pair(h))
            pl.when(differ)(lambda: rs_col.send_far(h))

        for h in range(PARTS + max(LATE_ROW, LATE_SUM)):
            if h < PARTS:
                early(h)
            if 0 <= h - LATE_SUM < PARTS:
                rs_col.combine(h - LATE_SUM)
            if 0 <= h - LATE_ROW < PARTS:
                late(h - LATE_ROW)

    @pl.when(s == 0)
    def _():
        load_ends.start()
        load_w.start()
        load_ends.wait()
        for h in parts:
            ag_col.own(h)[...] = ends_part(h)
        pl.semaphore_wait(barrier, greetings)
        for h in parts:
            ag_col.start(h)
        col_to_row()
        for h in parts:
            value, grad = gelu_pair(rs_row.finish(h))
            outgoing[h] = value.astype(jnp.bfloat16)
            cross_start(h)
            slope[h] = grad
            cross_slope(h).start()
        for h in parts:
            ag_col.drain(h)
            rs_row.drain(h)
            cross_drain(h)
            cross_slope(h).wait_send()
        for h in parts:
            cross(h).wait_recv()
            ag_row.start(h)
        row_to_col()
        weight_grad()
        for h in parts:
            ends_out[0, pl.ds(h * ROWS, ROWS), :] = rs_col.finish(h).astype(jnp.bfloat16)
        for h in parts:
            ag_row.drain(h)
            rs_col.drain(h)
        store_dw.wait()

    @pl.when(s == 1)
    def _():
        load_routes.start()
        load_ends.start()
        load_w.start()
        load_routes.wait()
        route_tiles[row.par, row.pos] = jnp.zeros((8, 128), jnp.float32)
        route_tiles[row.par, row.pos, 0:1, 0:2 * n] = route_row[...].astype(jnp.float32)
        load_ends.wait()
        pl.semaphore_wait(barrier, greetings)

        def tile_to(pos):
            mine = route_tiles.at[row.par, row.pos]
            return remote(mine, mine, rt_send.at[pos], rt_recv.at[row.pos], row.peer(pos))

        def tile_from(pos):
            tile = route_tiles.at[row.par, pos]
            return remote(tile, tile, rt_send.at[pos], rt_recv.at[pos], row.peer(pos))

        def tiles(par):
            return remote(route_tiles.at[par], route_tiles.at[par], rt_pair_send.at[0], rt_pair_recv.at[0], row.other(row.pos))

        row.peers(0, n - 1, lambda pos: tile_to(pos).start())
        row.peers(0, n - 1, lambda pos: tile_from(pos).wait_recv())
        tiles(row.par).start()
        tiles(1 - row.par).wait_recv()
        row.peers(0, n - 1, lambda pos: tile_to(pos).wait_send())
        tiles(row.par).wait_send()
        picked = route_tiles[col.par, col.pos, 0:1, :]
        lanes = lax.broadcasted_iota(jnp.int32, (1, 128), 1)
        routed = jnp.sum(jnp.where(lanes == r, picked, 0.0), axis=1, keepdims=True)

        for h in parts:
            cross(h).wait_recv()
            ag_row.start(h)
        row_to_col()
        for h in parts:
            value, grad = gelu_pair(rs_col.finish(h) * routed)
            masked = (ends_part(h).astype(jnp.float32) * grad).astype(jnp.bfloat16).astype(jnp.float32) * routed
            ag_col.own(h)[...] = masked.astype(jnp.bfloat16)
            ag_col.start(h)
            ends_out[0, pl.ds(h * ROWS, ROWS), :] = value.astype(jnp.bfloat16)
        col_to_row()
        for h in parts:
            grad_hidden = rs_row.finish(h).astype(jnp.bfloat16).astype(jnp.float32)
            cross_slope(h).wait_recv()
            outgoing[h] = (grad_hidden * slope[h]).astype(jnp.bfloat16)
            cross_start(h)
        weight_grad()
        for h in parts:
            ag_col.drain(h)
            rs_row.drain(h)
            ag_row.drain(h)
            rs_col.drain(h)
            cross_drain(h)
        store_dw.wait()


def shards(ends, weights, routes):
    width = weights.shape[1]
    n = lax.axis_size("row") // 2
    bf16, f32 = jnp.bfloat16, jnp.float32
    dma = pltpu.SemaphoreType.DMA
    anywhere = pl.BlockSpec(memory_space=pl.ANY)
    in_vmem = pl.BlockSpec(memory_space=pltpu.VMEM)
    lines = dma((2, PARTS, n))
    line = dma((PARTS, n))
    return pl.pallas_call(
        functools.partial(kernel, n),
        out_shape=(jax.ShapeDtypeStruct(ends.shape, bf16), jax.ShapeDtypeStruct(weights.shape, bf16)),
        in_specs=[anywhere, anywhere, anywhere],
        out_specs=(in_vmem, anywhere),
        scratch_shapes=[
            pltpu.VMEM((width, width), bf16),
            pltpu.VMEM(ends.shape[1:], bf16),
            pltpu.VMEM((PARTS, 2 * n, ROWS, width), bf16),
            pltpu.VMEM((PARTS, 2 * n, ROWS, width), bf16),
            pltpu.VMEM((PARTS, ROWS, width), bf16),
            pltpu.VMEM((PARTS, ROWS, width), f32),
            pltpu.VMEM(routes.shape, jnp.int32),
            pltpu.VMEM((2, n, 8, 128), f32),
            pltpu.VMEM((width, width), bf16),
            pltpu.VMEM((2, PARTS, 2, n, ROWS, width), bf16),
            pltpu.VMEM((2, PARTS, 2, n, ROWS, width), f32),
            pltpu.VMEM((2, PARTS, n, ROWS, width), bf16),
            pltpu.VMEM((2, PARTS, n, ROWS, width), bf16),
            pltpu.VMEM((2, PARTS, n, ROWS, width), bf16),
            pltpu.VMEM((PARTS, n, ROWS, width), bf16),
            lines, lines, lines, lines, lines,
            lines, lines, lines, lines, line, line,
            dma((PARTS,)), dma((PARTS,)), line, dma((PARTS,)), dma((PARTS,)),
            dma((n,)), dma((n,)), dma((1,)), dma((1,)), dma((4,)),
        ],
        compiler_params=pltpu.CompilerParams(
            collective_id=0, has_side_effects=True, vmem_limit_bytes=VMEM_LIMIT),
        cost_estimate=pl.CostEstimate(
            flops=24 * n * PARTS * ROWS * width * width, bytes_accessed=4 * width * width, transcendentals=0),
    )(ends, weights, routes)


def solution(mesh):
    placed = (P("section", "col", "row"), P("section", "row", "col"), P("row", None))
    return jax.shard_map(
        shards,
        mesh=mesh,
        in_specs=placed,
        out_specs=(P("section", "col", "row"), P("section", "row", "col")),
        check_vma=False,
    )
```

```python
import functools
import math

import jax
import jax.numpy as jnp
from jax import lax
from jax.experimental import pallas as pl
from jax.experimental.pallas import tpu as pltpu
from jax.sharding import PartitionSpec as P

MESH = pl.DeviceIdType.MESH
PARTS = 2
ROWS = 16
LATE_COL = 1
LATE_ROW = 0
LATE_SUM = 1
TILE = 256
FAR_GATHER = 0
FAR_SUM = 0
FAR_CROSS = 0
WHOLE_ROW_PAIR = True
VMEM_LIMIT = 62 * 2**20
GELU_SCALE = math.sqrt(2.0 / math.pi)
GELU_CUBE = 0.044715


def gelu_pair(x):
    square = x * x
    t = jnp.tanh(GELU_SCALE * (x + GELU_CUBE * x * square))
    cdf = 0.5 * (1.0 + t)
    inner = GELU_SCALE * (1.0 + 3.0 * GELU_CUBE * square)
    return x * cdf, cdf + 0.5 * x * (1.0 - t * t) * inner


def over(first, last, body):
    def step(i, carry):
        body(i)
        return carry

    if first < last:
        lax.fori_loop(first, last, step, 0, unroll=last - first < 9)


def remote(src, dst, send_sem, recv_sem, device):
    return pltpu.make_async_remote_copy(
        src_ref=src, dst_ref=dst, send_sem=send_sem, recv_sem=recv_sem,
        device_id=device, device_id_type=MESH)


class Line:
    def __init__(self, axis, n, place):
        self.n = n
        me = lax.axis_index(axis)
        self.pos = me // 2
        self.par = me % 2
        self.place = place

    def peer(self, pos):
        return self.place(pos * 2 + self.par)

    def other(self, pos):
        return self.place(pos * 2 + 1 - self.par)

    def at(self, i):
        j = (i + 1) // 2
        return lax.rem(self.pos + self.n // 2 + j * (1 - 2 * (i % 2)) + self.n, self.n)

    def peers(self, first, last, body):
        over(first, last, lambda i: body(self.at(i)))

    def peers_back(self, first, last, body):
        over(first, last, lambda i: body(self.at(first + last - 1 - i)))


class Gather:
    def __init__(self, line, buf, skip, far, ring_send, ring_recv, pair_send, pair_recv, far_send):
        self.line, self.buf, self.skip, self.far = line, buf, skip, far
        self.ring_send, self.ring_recv = ring_send, ring_recv
        self.pair_send, self.pair_recv = pair_send, pair_recv
        self.far_send = far_send

    def own(self, h):
        line = self.line
        return self.buf.at[h, line.par * line.n + line.pos]

    def ring(self, h, block_pos, peer_pos):
        line = self.line
        block = self.buf.at[h, line.par * line.n + block_pos]
        return remote(block, block, self.ring_send.at[h, peer_pos], self.ring_recv.at[h, block_pos], line.peer(peer_pos))

    def to_ring(self, h, pos):
        return self.ring(h, self.line.pos, pos)

    def from_ring(self, h, pos):
        return self.ring(h, pos, pos)

    def to_far(self, h, pos):
        line = self.line
        return remote(self.own(h), self.own(h), self.far_send.at[h, pos], self.pair_recv.at[h, line.pos], line.other(pos))

    def pair(self, h, par, pos):
        line = self.line
        block = self.buf.at[h, par * line.n + pos]
        return remote(block, block, self.pair_send.at[h, pos], self.pair_recv.at[h, pos], line.other(line.pos))

    def start(self, h):
        line = self.line

        def both(pos):
            self.to_ring(h, pos).start()
            self.to_far(h, pos).start()

        line.peers(self.skip, self.far, both)
        line.peers(max(self.skip, self.far), line.n - 1, lambda pos: self.to_ring(h, pos).start())
        self.pair(h, line.par, line.pos).start()

    def finish_ring(self, h):
        line = self.line

        def forward(pos):
            self.from_ring(h, pos).wait_recv()
            self.pair(h, line.par, pos).start()

        line.peers_back(self.far, line.n - 1, forward)
        line.peers_back(0, self.far, lambda pos: self.from_ring(h, pos).wait_recv())

    def finish_pair(self, h):
        line = self.line
        over(0, line.n, lambda pos: self.pair(h, 1 - line.par, pos).wait_recv())

    def drain(self, h):
        line = self.line
        line.peers(self.skip, line.n - 1, lambda pos: self.to_ring(h, pos).wait_send())
        line.peers(self.skip, self.far, lambda pos: self.to_far(h, pos).wait_send())
        line.peers(self.far, line.n - 1, lambda pos: self.pair(h, line.par, pos).wait_send())
        self.pair(h, line.par, line.pos).wait_send()


class Scatter:
    def __init__(self, line, far, whole, out, kept, got, both, land, far_land,
                 pair_send, pair_recv, ring_send, ring_recv, far_send, far_recv):
        self.line, self.far, self.whole = line, far, whole
        self.out, self.kept, self.got, self.both = out, kept, got, both
        self.land, self.far_land = land, far_land
        self.pair_send, self.pair_recv = pair_send, pair_recv
        self.ring_send, self.ring_recv = ring_send, ring_recv
        self.far_send, self.far_recv = far_send, far_recv

    def pair(self, h, pos):
        line = self.line
        if self.whole:
            return remote(self.out.at[h, 1 - line.par], self.got.at[h], self.pair_send.at[h, 0], self.pair_recv.at[h, 0], line.other(line.pos))
        return remote(self.out.at[h, 1 - line.par, pos], self.got.at[h, pos],
                      self.pair_send.at[h, pos], self.pair_recv.at[h, pos], line.other(line.pos))

    def ring(self, h, pos, land_pos):
        return remote(self.both.at[h, pos], self.land.at[h, land_pos],
                      self.ring_send.at[h, pos], self.ring_recv.at[h, land_pos], self.line.peer(pos))

    def to_ring(self, h, pos):
        return self.ring(h, pos, self.line.pos)

    def from_ring(self, h, pos):
        return self.ring(h, pos, pos)

    def direct(self, h, pos, land_pos):
        return remote(self.out.at[h, 1 - self.line.par, pos], self.far_land.at[h, land_pos],
                      self.far_send.at[h, pos], self.far_recv.at[h, land_pos], self.line.other(pos))

    def to_far(self, h, pos):
        return self.direct(h, pos, self.line.pos)

    def from_far(self, h, pos):
        return self.direct(h, pos, pos)

    def multiply(self, h, buf, w, transposed, par):
        n = self.line.n
        width = w.shape[0]
        tile = min(TILE, width)
        left = buf[h, pl.ds(par * n, n)].reshape(n * ROWS, width)

        def column(j):
            cut = pl.ds(j * tile, tile)
            if transposed:
                value = lax.dot_general(left, w[cut, :], (((1,), (1,)), ((), ())), preferred_element_type=jnp.float32)
            else:
                value = jnp.dot(left, w[:, cut], preferred_element_type=jnp.float32)
            self.kept[h, par, :, :, cut] = value.reshape(n, ROWS, tile)
            self.out[h, par, :, :, cut] = value.astype(jnp.bfloat16).reshape(n, ROWS, tile)

        for j in range(width // tile):
            column(j)

    def send_pair(self, h):
        line = self.line
        line.peers(0, self.far, lambda pos: self.to_far(h, pos).start())
        if not self.whole:
            line.peers(self.far, line.n - 1, lambda pos: self.pair(h, pos).start())
        self.pair(h, line.pos).start()

    def send_far(self, h):
        line = self.line

        def send(pos):
            self.both[h, pos, :] = self.out[h, line.par, pos, :]
            self.to_ring(h, pos).start()

        line.peers(0, self.far, send)

    def combine(self, h):
        line = self.line
        if self.whole:
            self.pair(h, 0).wait_recv()

        def send(pos):
            if not self.whole:
                self.pair(h, pos).wait_recv()
            total = self.kept[h, line.par, pos, :] + self.got[h, pos, :].astype(jnp.float32)
            self.both[h, pos, :] = total.astype(jnp.bfloat16)
            self.to_ring(h, pos).start()

        line.peers(self.far, line.n - 1, send)

    def finish(self, h):
        line = self.line
        if not self.whole:
            self.pair(h, line.pos).wait_recv()
        total = self.kept[h, line.par, line.pos, :] + self.got[h, line.pos, :].astype(jnp.float32)

        def near(i, total):
            pos = line.at(line.n - 2 - i)
            self.from_ring(h, pos).wait_recv()
            return total + self.land[h, pos, :].astype(jnp.float32)

        total = lax.fori_loop(0, line.n - 1, near, total, unroll=True)

        def far(i, total):
            pos = line.at(self.far - 1 - i)
            self.from_far(h, pos).wait_recv()
            return total + self.far_land[h, pos, :].astype(jnp.float32)

        return lax.fori_loop(0, self.far, far, total) if self.far else total

    def drain(self, h):
        line = self.line
        if not self.whole:
            line.peers(self.far, line.n - 1, lambda pos: self.pair(h, pos).wait_send())
        self.pair(h, line.pos).wait_send()
        line.peers(0, line.n - 1, lambda pos: self.to_ring(h, pos).wait_send())
        line.peers(0, self.far, lambda pos: self.to_far(h, pos).wait_send())


def kernel(n, ends_hbm, w_hbm, routes_hbm, ends_out, dw_hbm,
           w, ends, col_buf, row_buf, outgoing, slope, route_row, route_tiles, dw,
           rs_out, rs_kept, rs_got, rs_both, rs_land, rs_far_land,
           ag_ring_send, ag_ring_recv, ag_pair_send, ag_pair_recv, ag_far_send,
           rs_ring_send, rs_ring_recv, rs_pair_send, rs_pair_recv, rs_far_send, rs_far_recv,
           cross_send, cross_recv, cross_far_send, slope_send, slope_recv,
           rt_send, rt_recv, rt_pair_send, rt_pair_recv, local_sem):
    s, r, c = lax.axis_index("section"), lax.axis_index("row"), lax.axis_index("col")
    row = Line("row", n, lambda i: (s, i, c))
    col = Line("col", n, lambda i: (s, r, i))
    over_there = (1 - s, r, c)
    far_gather, far_sum, far_cross = (min(far, n - 1) for far in (FAR_GATHER, FAR_SUM, FAR_CROSS))
    parts = range(PARTS)

    def gather(line, buf, skip, far, k):
        return Gather(line, buf, skip, far, ag_ring_send.at[k], ag_ring_recv.at[k],
                      ag_pair_send.at[k], ag_pair_recv.at[k], ag_far_send.at[k])

    ag_col = gather(col, col_buf, 0, far_gather, 0)
    ag_row = gather(row, row_buf, far_cross, 0, 1)

    def scatter(line, far, whole, k):
        return Scatter(line, far, whole, rs_out.at[k], rs_kept.at[k], rs_got.at[k], rs_both.at[k],
                       rs_land.at[k], rs_far_land, rs_pair_send.at[k], rs_pair_recv.at[k],
                       rs_ring_send.at[k], rs_ring_recv.at[k], rs_far_send, rs_far_recv)

    rs_row, rs_col = scatter(row, 0, WHOLE_ROW_PAIR, 0), scatter(col, far_sum, False, 1)

    def cross(h):
        return remote(outgoing.at[h], ag_row.own(h), cross_send.at[h], cross_recv.at[h], over_there)

    def cross_far(h, pos):
        return remote(outgoing.at[h], ag_row.own(h), cross_far_send.at[h, pos],
                      ag_row.ring_recv.at[h, row.pos], (1 - s, pos * 2 + row.par, c))

    def cross_slope(h):
        return remote(slope.at[h], slope.at[h], slope_send.at[h], slope_recv.at[h], over_there)

    def cross_start(h):
        cross(h).start()
        row.peers(0, far_cross, lambda pos: cross_far(h, pos).start())

    def cross_drain(h):
        cross(h).wait_send()
        row.peers(0, far_cross, lambda pos: cross_far(h, pos).wait_send())

    load_w = pltpu.make_async_copy(w_hbm.at[0], w, local_sem.at[0])
    store_dw = pltpu.make_async_copy(dw, dw_hbm.at[0], local_sem.at[1])
    load_routes = pltpu.make_async_copy(routes_hbm, route_row, local_sem.at[3])

    load_ends = pltpu.make_async_copy(ends_hbm.at[0], ends, local_sem.at[2])

    def ends_part(h):
        return ends[pl.ds(h * ROWS, ROWS), :]

    barrier = pltpu.get_barrier_semaphore()

    def greet(device):
        pl.semaphore_signal(barrier, inc=1, device_id=device, device_id_type=MESH)

    far_col = max(far_gather, far_sum)
    col.peers(0, n - 1, lambda pos: greet(col.peer(pos)))
    col.peers(0, far_col, lambda pos: greet(col.other(pos)))
    greet(col.other(col.pos))
    row.peers(0, n - 1, lambda pos: greet(row.peer(pos)))
    greet(row.other(row.pos))
    greet(over_there)
    row.peers(0, far_cross, lambda pos: greet((1 - s, pos * 2 + row.par, c)))
    greetings = 2 * (n - 1) + 3 + far_col + far_cross

    def weight_grad():
        width = w.shape[0]
        tile = min(TILE, width)

        def block(k):
            at_row = pl.ds(pl.multiple_of((k // (width // tile)) * tile, tile), tile)
            at_col = pl.ds(pl.multiple_of((k % (width // tile)) * tile, tile), tile)
            total = jnp.zeros((tile, tile), jnp.float32)
            for h in parts:
                total = total + lax.dot_general(
                    col_buf[h, :, :, at_row].reshape(-1, tile), row_buf[h, :, :, at_col].reshape(-1, tile),
                    (((0,), (0,)), ((), ())),
                    preferred_element_type=jnp.float32)
            dw[at_row, at_col] = total.astype(jnp.bfloat16)

        over(0, (width // tile) ** 2, block)
        store_dw.start()

    same = row.par == col.par
    differ = row.par != col.par

    def staggered(early, late, lag):
        for h in range(PARTS + lag):
            if h < PARTS:
                early(h)
            if h >= lag:
                late(h - lag)

    def col_to_row():
        def early(h):
            ag_col.finish_ring(h)
            if h == 0:
                pl.when(s == 0)(load_w.wait)
            rs_row.multiply(h, col_buf, w, False, col.par)
            pl.when(differ)(lambda: rs_row.send_pair(h))
            pl.when(same)(lambda: rs_row.combine(h))

        def late(h):
            ag_col.finish_pair(h)
            rs_row.multiply(h, col_buf, w, False, 1 - col.par)
            pl.when(same)(lambda: rs_row.send_pair(h))
            pl.when(differ)(lambda: rs_row.combine(h))

        staggered(early, late, LATE_COL)

    def row_to_col():
        def early(h):
            ag_row.finish_ring(h)
            if h == 0:
                pl.when(s == 1)(load_w.wait)
            rs_col.multiply(h, row_buf, w, True, row.par)
            pl.when(differ)(lambda: rs_col.send_pair(h))
            pl.when(same)(lambda: rs_col.send_far(h))

        def late(h):
            ag_row.finish_pair(h)
            rs_col.multiply(h, row_buf, w, True, 1 - row.par)
            pl.when(same)(lambda: rs_col.send_pair(h))
            pl.when(differ)(lambda: rs_col.send_far(h))

        for h in range(PARTS + max(LATE_ROW, LATE_SUM)):
            if h < PARTS:
                early(h)
            if 0 <= h - LATE_SUM < PARTS:
                rs_col.combine(h - LATE_SUM)
            if 0 <= h - LATE_ROW < PARTS:
                late(h - LATE_ROW)

    @pl.when(s == 0)
    def _():
        load_ends.start()
        load_w.start()
        load_ends.wait()
        for h in parts:
            ag_col.own(h)[...] = ends_part(h)
        pl.semaphore_wait(barrier, greetings)
        for h in parts:
            ag_col.start(h)
        col_to_row()
        for h in parts:
            value, grad = gelu_pair(rs_row.finish(h))
            outgoing[h] = value.astype(jnp.bfloat16)
            cross_start(h)
            slope[h] = grad
            cross_slope(h).start()
        for h in parts:
            ag_col.drain(h)
            rs_row.drain(h)
            cross_drain(h)
            cross_slope(h).wait_send()
        for h in parts:
            cross(h).wait_recv()
            ag_row.start(h)
        row_to_col()
        weight_grad()
        for h in parts:
            ag_row.drain(h)
            rs_col.drain(h)
        store_dw.wait()
        for h in parts:
            ends_out[0, pl.ds(h * ROWS, ROWS), :] = rs_col.finish(h).astype(jnp.bfloat16)

    @pl.when(s == 1)
    def _():
        load_routes.start()
        load_ends.start()
        load_w.start()
        load_routes.wait()
        route_tiles[row.par, row.pos] = jnp.zeros((8, 128), jnp.float32)
        route_tiles[row.par, row.pos, 0:1, 0:2 * n] = route_row[...].astype(jnp.float32)
        load_ends.wait()
        pl.semaphore_wait(barrier, greetings)

        def tile_to(pos):
            mine = route_tiles.at[row.par, row.pos]
            return remote(mine, mine, rt_send.at[pos], rt_recv.at[row.pos], row.peer(pos))

        def tile_from(pos):
            tile = route_tiles.at[row.par, pos]
            return remote(tile, tile, rt_send.at[pos], rt_recv.at[pos], row.peer(pos))

        def tiles(par):
            return remote(route_tiles.at[par], route_tiles.at[par], rt_pair_send.at[0], rt_pair_recv.at[0], row.other(row.pos))

        row.peers(0, n - 1, lambda pos: tile_to(pos).start())
        row.peers(0, n - 1, lambda pos: tile_from(pos).wait_recv())
        tiles(row.par).start()
        tiles(1 - row.par).wait_recv()
        row.peers(0, n - 1, lambda pos: tile_to(pos).wait_send())
        tiles(row.par).wait_send()
        picked = route_tiles[col.par, col.pos, 0:1, :]
        lanes = lax.broadcasted_iota(jnp.int32, (1, 128), 1)
        routed = jnp.sum(jnp.where(lanes == r, picked, 0.0), axis=1, keepdims=True)

        for h in parts:
            cross(h).wait_recv()
            ag_row.start(h)
        row_to_col()
        for h in parts:
            value, grad = gelu_pair(rs_col.finish(h) * routed)
            masked = (ends_part(h).astype(jnp.float32) * grad).astype(jnp.bfloat16).astype(jnp.float32) * routed
            ag_col.own(h)[...] = masked.astype(jnp.bfloat16)
            ag_col.start(h)
            ends_out[0, pl.ds(h * ROWS, ROWS), :] = value.astype(jnp.bfloat16)
        col_to_row()
        for h in parts:
            grad_hidden = rs_row.finish(h).astype(jnp.bfloat16).astype(jnp.float32)
            cross_slope(h).wait_recv()
            outgoing[h] = (grad_hidden * slope[h]).astype(jnp.bfloat16)
            cross_start(h)
        weight_grad()
        for h in parts:
            ag_col.drain(h)
            rs_row.drain(h)
            ag_row.drain(h)
            rs_col.drain(h)
            cross_drain(h)
        store_dw.wait()


def shards(ends, weights, routes):
    width = weights.shape[1]
    n = lax.axis_size("row") // 2
    bf16, f32 = jnp.bfloat16, jnp.float32
    dma = pltpu.SemaphoreType.DMA
    anywhere = pl.BlockSpec(memory_space=pl.ANY)
    in_vmem = pl.BlockSpec(memory_space=pltpu.VMEM)
    lines = dma((2, PARTS, n))
    line = dma((PARTS, n))
    return pl.pallas_call(
        functools.partial(kernel, n),
        out_shape=(jax.ShapeDtypeStruct(ends.shape, bf16), jax.ShapeDtypeStruct(weights.shape, bf16)),
        in_specs=[anywhere, anywhere, anywhere],
        out_specs=(in_vmem, anywhere),
        scratch_shapes=[
            pltpu.VMEM((width, width), bf16),
            pltpu.VMEM(ends.shape[1:], bf16),
            pltpu.VMEM((PARTS, 2 * n, ROWS, width), bf16),
            pltpu.VMEM((PARTS, 2 * n, ROWS, width), bf16),
            pltpu.VMEM((PARTS, ROWS, width), bf16),
            pltpu.VMEM((PARTS, ROWS, width), f32),
            pltpu.VMEM(routes.shape, jnp.int32),
            pltpu.VMEM((2, n, 8, 128), f32),
            pltpu.VMEM((width, width), bf16),
            pltpu.VMEM((2, PARTS, 2, n, ROWS, width), bf16),
            pltpu.VMEM((2, PARTS, 2, n, ROWS, width), f32),
            pltpu.VMEM((2, PARTS, n, ROWS, width), bf16),
            pltpu.VMEM((2, PARTS, n, ROWS, width), bf16),
            pltpu.VMEM((2, PARTS, n, ROWS, width), bf16),
            pltpu.VMEM((PARTS, n, ROWS, width), bf16),
            lines, lines, lines, lines, lines,
            lines, lines, lines, lines, line, line,
            dma((PARTS,)), dma((PARTS,)), line, dma((PARTS,)), dma((PARTS,)),
            dma((n,)), dma((n,)), dma((1,)), dma((1,)), dma((4,)),
        ],
        compiler_params=pltpu.CompilerParams(
            collective_id=0, has_side_effects=True, vmem_limit_bytes=VMEM_LIMIT),
        cost_estimate=pl.CostEstimate(
            flops=24 * n * PARTS * ROWS * width * width, bytes_accessed=4 * width * width, transcendentals=0),
    )(ends, weights, routes)


def solution(mesh):
    placed = (P("section", "col", "row"), P("section", "row", "col"), P("row", None))
    return jax.shard_map(
        shards,
        mesh=mesh,
        in_specs=placed,
        out_specs=(P("section", "col", "row"), P("section", "row", "col")),
        check_vma=False,
    )
```
